1024 devices in a mesh: grp: 128 (over x, z), dev: 8 (over y, core).
Axes of the slice: x: 4, y: 4, z: 32, core: 2. Of those that a mesh axis runs over, the one named last changes fastest.
Arguments:
- features: bfloat16 [262144, 256], P(('grp', 'dev')), may hold values from -6 to 6
- tiles: bfloat16 [8192, 128, 128], P(('grp', 'dev')), may hold values from -0.375 to 0.375
- tile_dst: int32 [8192], P(('grp', 'dev')), may hold values from 0 to 1
- tile_src: int32 [8192], P(('grp', 'dev')), may hold values from 0 to 31
- tile_count: int32 [1024], P(('grp', 'dev')), may hold values from 1 to 8, as said below
- send_rows: int32 [1024, 128, 2], P(('grp', 'dev')), may hold values from 0 to 255, as said below
- send_count: int32 [1024, 128], P(('grp', 'dev')), may hold values from 0 to 2, as said below
- weight: bfloat16 [256, 256], replicated, may hold values from -0.375 to 0.375
- cotangent: bfloat16 [262144, 256], P(('grp', 'dev')), may hold values from -6 to 6
Outputs:
- output: bfloat16 [262144, 256], P(('grp', 'dev'))
- grad_features: float32 [262144, 256], P(('grp', 'dev'))
- grad_weight: float32 [256, 256], replicated
The draws below stay inside these ranges and needn't reach their ends.
Inputs may be any that keep to these rules, and one draw needn't show every extreme that they name: The first tile_count entries of a device's tile lists are used, the others ignored; some device has 8. `send_rows`: local row numbers of the sending device, distinct within each list of one device for one peer group. The first send_count entries of a list are live; some group receives 2 live rows from every device.
All inputs are finite; a program needn't handle non-finite values.
Results may differ from the reference program's by a relative error of at most 0.013.
Values may be sent and summed in bfloat16 or wider, within the bound.
No kernel may reach another device: no remote copies, remote signals or barrier semaphores. Data moves between devices by JAX's collectives and lax.ppermute only.
A program may use at most 32 MiB of HBM per device.

```python
import jax
import jax.numpy as jnp
from jax import lax

F = 256
ROWS_DEV = 256
TILE = 128
NT = 8
SEND = 2
GROUPS = 128
MEMBERS = 8
NODES = 262144
RT = 2
BOUND = 2048
SRC_TILES = 32


def draw_tile_count(key, part):
    key = jax.random.fold_in(key, 11)
    key_shift, key_full = jax.random.split(key)
    shifts = jax.random.randint(key_shift, (GROUPS * MEMBERS,), 0, 4)
    counts = jnp.maximum(jnp.right_shift(jnp.int32(NT), shifts.astype(jnp.int32)), 1)
    chosen = jax.random.randint(key_full, (), 0, GROUPS * MEMBERS)
    return counts.at[chosen].set(NT).astype(jnp.int32)


def draw_send_rows(key, part):
    key = jax.random.fold_in(key, 12)
    scores = jax.random.randint(key, (GROUPS * MEMBERS, GROUPS, ROWS_DEV), 0, 1 << 20)
    scores = scores * ROWS_DEV + jnp.arange(ROWS_DEV, dtype=jnp.int32)
    return lax.top_k(scores, SEND)[1].astype(jnp.int32)


def draw_send_count(key, part):
    key = jax.random.fold_in(key, 13)
    key_count, key_column = jax.random.split(key)
    counts = jax.random.randint(key_count, (GROUPS * MEMBERS, GROUPS), 0, SEND + 1)
    column = jax.random.randint(key_column, (), 0, GROUPS)
    return counts.at[:, column].set(SEND).astype(jnp.int32)


def with_ends(entries, own_key, low, top_value):
    longest = entries.shape.index(max(entries.shape))
    spots = []
    for shift in (0, 1):
        where = [jax.random.randint(jax.random.fold_in(own_key, axis), (), 0, length) for axis, length in enumerate(entries.shape)]
        where[longest] = (where[longest] + shift) % entries.shape[longest]
        spots.append(tuple(where))
    return entries.at[spots[0]].set(low).at[spots[1]].set(top_value)


def block_scale(stream_key, dims, cuts, least, high):
    loudness, own = 1.0, jax.random.fold_in(stream_key, 6)
    for dim, parts in cuts:
        steps = jnp.exp(jax.random.uniform(jax.random.fold_in(own, dim), (parts,), jnp.float32, least / len(cuts), high / len(cuts)))
        loudness = loudness * jnp.repeat(steps, dims[dim] // parts).reshape([-1 if axis == dim else 1 for axis in range(len(dims))])
    return loudness


def scatter_about(own_key, extent, width, reach, cuts=(), held_as=jnp.bfloat16):
    drawn = width * jax.random.normal(own_key, extent, jnp.float32)
    if cuts:
        drawn = drawn * block_scale(own_key, extent, cuts, -0.22, 0.18)
    return jnp.clip(drawn, -reach, reach).astype(held_as)


def setup_inputs(seed: int = 0) -> dict:
    key_list = jax.random.split(jax.random.key(seed), 10)
    features = scatter_about(key_list[0], (NODES, F), 1.0, 6.0, ((0, 1024),))
    tiles = scatter_about(key_list[1], (GROUPS * MEMBERS * NT, TILE, TILE), (TILE * NT // (2 * RT)) ** -0.5, 0.375, ((0, 1024),))
    tile_dst = with_ends(jax.random.randint(key_list[2], (GROUPS * MEMBERS * NT,), 0, RT), jax.random.fold_in(key_list[2], 1), 0, RT - 1).astype(jnp.int32)
    tile_src = with_ends(jax.random.randint(key_list[3], (GROUPS * MEMBERS * NT,), 0, SRC_TILES), jax.random.fold_in(key_list[3], 1), 0, SRC_TILES - 1).astype(jnp.int32)
    tile_count = draw_tile_count(jax.random.fold_in(key_list[9], 71), 0)
    send_rows = draw_send_rows(jax.random.fold_in(key_list[9], 71), 0)
    send_count = draw_send_count(jax.random.fold_in(key_list[9], 71), 0)
    weight = scatter_about(key_list[7], (F, F), F ** -0.5, 0.375)
    cotangent = scatter_about(key_list[8], (NODES, F), 1.0, 6.0, ((0, 1024),))
    return dict(features=features, tiles=tiles, tile_dst=tile_dst, tile_src=tile_src, tile_count=tile_count, send_rows=send_rows, send_count=send_count, weight=weight, cotangent=cotangent)


def wanted_rows(features, send_rows, send_count):
    owned = features.reshape(GROUPS * MEMBERS, ROWS_DEV, F)
    picked = jax.vmap(lambda own_rows, row_index: own_rows[row_index])(owned, send_rows)
    live_slots = jnp.arange(SEND, dtype=jnp.int32)[None, None, :] < send_count[:, :, None]
    outgoing = jnp.where(live_slots[..., None], picked, jnp.zeros_like(picked))
    return outgoing, live_slots


def reference(features, tiles, tile_dst, tile_src, tile_count, send_rows, send_count, weight, cotangent):
    outgoing, live_slots = wanted_rows(features, send_rows, send_count)
    grouped = outgoing.reshape(GROUPS, MEMBERS, GROUPS, SEND, F).transpose(2, 1, 0, 3, 4).reshape(GROUPS, BOUND, F)
    padding = SRC_TILES * TILE - MEMBERS * ROWS_DEV - BOUND
    sources = jnp.concatenate([features.reshape(GROUPS, MEMBERS * ROWS_DEV, F), grouped,
                               jnp.zeros((GROUPS, padding, F), jnp.bfloat16)], axis=1)
    tile_sets = tiles.reshape(GROUPS * MEMBERS, NT, TILE, TILE)
    dest_sets = tile_dst.reshape(GROUPS * MEMBERS, NT)
    source_sets = tile_src.reshape(GROUPS * MEMBERS, NT)
    slot_index = jnp.arange(NT, dtype=jnp.int32)
    dest_index = jnp.arange(RT, dtype=jnp.int32)

    def forward_device(device_index):
        group_index = device_index // MEMBERS
        blocks = sources[group_index].reshape(SRC_TILES, TILE, F)[source_sets[device_index]]
        products = jnp.einsum('kij,kjf->kif', tile_sets[device_index].astype(jnp.float32), blocks.astype(jnp.float32))
        live_tiles = slot_index < tile_count[device_index]
        selector = ((dest_sets[device_index][None, :] == dest_index[:, None]) & live_tiles[None, :]).astype(jnp.float32)
        summed = jnp.einsum('tk,kif->tif', selector, products, precision=lax.Precision.HIGHEST)
        return summed.reshape(ROWS_DEV, F).astype(jnp.bfloat16)

    aggregated = lax.map(forward_device, jnp.arange(GROUPS * MEMBERS, dtype=jnp.int32)).reshape(NODES, F)
    output = jnp.dot(aggregated, weight, preferred_element_type=jnp.float32).astype(jnp.bfloat16)
    grad_weight = jnp.dot(aggregated.T, cotangent, preferred_element_type=jnp.float32)
    upstream = jnp.dot(cotangent, weight.T, preferred_element_type=jnp.float32).astype(jnp.bfloat16)
    up_sets = upstream.reshape(GROUPS * MEMBERS, RT, TILE, F)

    def backward_group(group_index):
        def member_terms(member_index):
            device_index = group_index * MEMBERS + member_index
            dest_rows = up_sets[device_index][dest_sets[device_index]]
            contrib = jnp.einsum('kji,kjf->kif', tile_sets[device_index].astype(jnp.float32), dest_rows.astype(jnp.float32))
            live_tiles = slot_index < tile_count[device_index]
            contrib = jnp.where(live_tiles[:, None, None], contrib, jnp.float32(0.0))
            partial_terms = jnp.zeros((SRC_TILES, TILE, F), jnp.float32).at[source_sets[device_index]].add(contrib)
            return partial_terms.astype(jnp.bfloat16)

        member_parts = jax.vmap(member_terms)(jnp.arange(MEMBERS, dtype=jnp.int32))
        summed = jnp.sum(member_parts.astype(jnp.float32), axis=0).reshape(SRC_TILES * TILE, F)
        return summed[:MEMBERS * ROWS_DEV + BOUND]

    summed_all = lax.map(backward_group, jnp.arange(GROUPS, dtype=jnp.int32))
    local_grads = summed_all[:, :MEMBERS * ROWS_DEV].reshape(NODES, F)
    returned = summed_all[:, MEMBERS * ROWS_DEV:].astype(jnp.bfloat16)
    returned = returned.reshape(GROUPS, MEMBERS, GROUPS, SEND, F).transpose(2, 1, 0, 3, 4).reshape(GROUPS * MEMBERS, GROUPS, SEND, F)

    def scatter_device(arrived, row_index, keep_mask):
        values = jnp.where(keep_mask[..., None], arrived.astype(jnp.float32), jnp.float32(0.0))
        return jnp.zeros((ROWS_DEV, F), jnp.float32).at[row_index.reshape(-1)].add(values.reshape(-1, F))

    added = jax.vmap(scatter_device)(returned, send_rows, live_slots).reshape(NODES, F)
    grad_features = local_grads + added
    return output, grad_features, grad_weight
```

```python
import jax
import jax.numpy as jnp
from jax import lax
from jax.experimental import pallas as pl
from jax.experimental.pallas import tpu as pltpu
from jax.sharding import Mesh, PartitionSpec as P

AXES = ("x", "zh", "zl", "y", "core")
SIZES = (4, 16, 2, 4, 2)
GRP = ("x", "zh", "zl")
DEV = ("y", "core")
NEAR = ("x", "zl", "y", "core")
FAR = "zh"
MEMBERS = 8
NEAR_SIZE = 64
FAR_SIZE = 16
TILE = 128
NT = 8

F32 = jnp.float32
BF16 = jnp.bfloat16
SMEM = pl.BlockSpec(memory_space=pltpu.SMEM)
VMEM = pl.BlockSpec(memory_space=pltpu.VMEM)


def swap(x, axes):
    return lax.all_to_all(x, axes, split_axis=0, concat_axis=0, tiled=True)


def dot(a, b, da=1, db=0):
    return lax.dot_general(a, b, (((da,), (db,)), ((), ())), preferred_element_type=F32)


def halves(x):
    high = x.astype(BF16)
    return high, (x - high.astype(F32)).astype(BF16)


def params():
    return pltpu.CompilerParams(vmem_limit_bytes=24 * 1024 * 1024)


def one_hot(idx_ref, rows):
    slots = idx_ref.shape[1]
    places = lax.broadcasted_iota(jnp.int32, (rows, slots), 0)
    return (places == idx_ref[...]).astype(F32).astype(BF16)


def pick_kernel(idx_ref, features_ref, out_ref):
    picks = one_hot(idx_ref, features_ref.shape[0])
    out_ref[...] = dot(picks, features_ref[...], 0, 0).astype(BF16)


def terms_kernel(count_ref, src_ref, dst_ref, tiles_ref, cot_ref, out_ref, acc_ref):
    live = count_ref[0]
    out_ref[...] = jnp.zeros(out_ref.shape, BF16)
    for k in range(NT):
        @pl.when(k < live)
        def _():
            acc_ref[src_ref[k]] = jnp.zeros(acc_ref.shape[1:], F32)
    for k in range(NT):
        @pl.when(k < live)
        def _():
            acc_ref[src_ref[k]] += dot(tiles_ref[k], cot_ref[dst_ref[k]], 0, 0)
    for k in range(NT):
        @pl.when(k < live)
        def _():
            block = src_ref[k]
            member = (block % 16) // 2
            part = block % 2 + 2 * (block // 16)
            out_ref[member, part] = acc_ref[block].astype(BF16)


def mid_kernel(terms_ref, features_ref, arrived_ref, own_ref, bound_ref, gw_ref):
    own = terms_ref[0, 0].astype(F32)
    bound = terms_ref[0, 1].astype(F32)
    for m in range(1, MEMBERS):
        own += terms_ref[m, 0].astype(F32)
        bound += terms_ref[m, 1].astype(F32)
    own_ref[...] = own
    bound_ref[...] = bound.astype(BF16)
    own_high, own_low = halves(own)
    bound_high, bound_low = halves(bound)
    features = features_ref[...]
    arrived = arrived_ref[...]
    gw_ref[...] = (dot(features, own_high, 0, 0) + dot(features, own_low, 0, 0)
                   + dot(arrived, bound_high, 0, 0) + dot(arrived, bound_low, 0, 0))


def forward_kernel(count_ref, src_ref, dst_ref, tiles_ref, own_ref, bound_ref, weight_ref, out_ref, acc_ref):
    live = count_ref[0]
    acc_ref[...] = jnp.zeros(acc_ref.shape, F32)
    for k in range(NT):
        block = src_ref[k]

        @pl.when((k < live) & (block < 16))
        def _():
            acc_ref[dst_ref[k]] += dot(tiles_ref[k], own_ref[block])

        @pl.when((k < live) & (block >= 16))
        def _():
            acc_ref[dst_ref[k]] += dot(tiles_ref[k], bound_ref[block - 16])
    for t in range(2):
        out_ref[t] = dot(acc_ref[t].astype(BF16), weight_ref[...]).astype(BF16)


def back_kernel(idx_ref, own_ref, back_ref, weight_ref, out_ref):
    picks = one_hot(idx_ref, own_ref.shape[0])
    total = own_ref[...] + dot(picks, back_ref[...])
    high, low = halves(total)
    weight = weight_ref[...]
    out_ref[...] = dot(high, weight, 1, 1) + dot(low, weight, 1, 1)


def per_device(
    features, tiles, tile_dst, tile_src, tile_count, send_rows, send_count, weight, cotangent
):
    rows, width = features.shape
    groups, slots = send_rows.shape[1:]
    shape = jax.ShapeDtypeStruct
    live = jnp.arange(slots, dtype=jnp.int32)[None, :] < send_count[0][:, None]
    idx = jnp.where(live, send_rows[0], -1).reshape(1, groups * slots)

    outgoing = pl.pallas_call(
        pick_kernel, out_shape=shape((groups * slots, width), BF16),
        in_specs=[VMEM, VMEM], out_specs=VMEM, compiler_params=params(), name="pick",
    )(idx, features)
    arrived = swap(outgoing.reshape(groups, slots, width), GRP).reshape(groups * slots, width)

    terms = pl.pallas_call(
        terms_kernel, out_shape=shape((MEMBERS, 4, TILE, width), BF16),
        in_specs=[SMEM, SMEM, SMEM, VMEM, VMEM], out_specs=VMEM,
        scratch_shapes=[pltpu.VMEM((32, TILE, width), F32)],
        compiler_params=params(), name="terms",
    )(tile_count, tile_src, tile_dst, tiles, cotangent.reshape(2, TILE, width))
    terms = swap(terms, DEV).reshape(MEMBERS, 2, rows, width)

    own, bound, gw = pl.pallas_call(
        mid_kernel,
        out_shape=(shape((rows, width), F32), shape((rows, width), BF16), shape((width, width), F32)),
        in_specs=[VMEM] * 3, out_specs=(VMEM,) * 3, compiler_params=params(), name="mid",
    )(terms, features, arrived)

    near = swap(gw.reshape(NEAR_SIZE, width // NEAR_SIZE, width), NEAR).sum(axis=0)
    far = swap(jnp.broadcast_to(near[None], (FAR_SIZE,) + near.shape), FAR).sum(axis=0)
    grad_weight = swap(jnp.broadcast_to(far[None], (NEAR_SIZE,) + far.shape), NEAR).reshape(width, width)

    back = swap(bound.reshape(groups, slots, width), GRP).reshape(groups * slots, width)
    grad_features = pl.pallas_call(
        back_kernel, out_shape=shape((rows, width), F32),
        in_specs=[VMEM] * 4, out_specs=VMEM, compiler_params=params(), name="back",
    )(idx, own, back, weight)

    all_own = lax.all_gather(features, DEV, axis=0, tiled=True)
    all_bound = lax.all_gather(arrived, DEV, axis=0, tiled=True)
    output = pl.pallas_call(
        forward_kernel, out_shape=shape((2, TILE, width), BF16),
        in_specs=[SMEM, SMEM, SMEM, VMEM, VMEM, VMEM, VMEM], out_specs=VMEM,
        scratch_shapes=[pltpu.VMEM((2, TILE, width), F32)],
        compiler_params=params(), name="forward",
    )(tile_count, tile_src, tile_dst, tiles, all_own.reshape(16, TILE, width),
      all_bound.reshape(16, TILE, width), weight).reshape(rows, width)
    return output, grad_features, grad_weight


def solution(mesh):
    fine = Mesh(mesh.devices.reshape(SIZES), AXES)
    placed = (
        P(AXES, None),
        P(AXES, None, None),
        P(AXES),
        P(AXES),
        P(AXES),
        P(AXES, None, None),
        P(AXES, None),
        P(),
        P(AXES, None),
    )
    return jax.shard_map(
        per_device,
        mesh=fine,
        in_specs=placed,
        out_specs=(P(AXES, None), P(AXES, None), P()),
        check_vma=False,
    )
```

```python
import jax
import jax.numpy as jnp
from jax import lax
from jax.experimental import pallas as pl
from jax.experimental.pallas import tpu as pltpu
from jax.sharding import Mesh, PartitionSpec as P

AXES = ("x", "zh", "zl", "y", "core")
SIZES = (4, 16, 2, 4, 2)
SLOTS = 2
X, ZH, ZL, Y, CORE = SIZES
GRP = ("x", "zh", "zl")
DEV = ("y", "core")
SIDE = ("x", "zl")
NEAR = ("x", "zl", "y", "core")
FAR = "zh"
TILE = 128
NT = 8
CHUNKS = 64

F32 = jnp.float32
BF16 = jnp.bfloat16
SMEM = pl.BlockSpec(memory_space=pltpu.SMEM)
ANY = pl.BlockSpec(memory_space=pl.ANY)
VMEM = pl.BlockSpec(memory_space=pltpu.VMEM)


def swap(x, axes):
    return lax.all_to_all(x, axes, split_axis=0, concat_axis=0, tiled=True)


def shift(x, axis, step, size):
    return lax.ppermute(x, axis, [(i, (i + step) % size) for i in range(size)])


def dot(a, b, da=1, db=0):
    return lax.dot_general(a, b, (((da,), (db,)), ((), ())), preferred_element_type=F32)


def halves(x):
    high = x.astype(BF16)
    return high, (x - high.astype(F32)).astype(BF16)


def call(kernel, out_shape, in_specs, name, scratch=()):
    out_specs = (VMEM,) * len(out_shape) if isinstance(out_shape, tuple) else VMEM
    return pl.pallas_call(
        kernel, out_shape=out_shape, in_specs=in_specs, out_specs=out_specs,
        scratch_shapes=scratch, name=name,
        compiler_params=pltpu.CompilerParams(vmem_limit_bytes=24 * 1024 * 1024),
    )


def one_hot(idx_ref, rows):
    places = lax.broadcasted_iota(jnp.int32, (rows, idx_ref.shape[1]), 0)
    return (places == idx_ref[...]).astype(F32).astype(BF16)


def digits(count, dim, sizes):
    left = lax.broadcasted_iota(jnp.int32, (count, count), dim)
    found = []
    for size in reversed(sizes):
        found.append(lax.rem(left, size))
        left = lax.div(left, size)
    return found[::-1]


def boundary_row(x, zh, zl, s):
    return ((x * ZH + zh) * ZL + zl) * SLOTS + s


def permutation(match):
    return match.astype(F32).astype(BF16)


def pick_kernel(idx_ref, features_ref, out_ref):
    picks = one_hot(idx_ref, features_ref.shape[0])
    out_ref[...] = dot(picks, features_ref[...], 0, 0).astype(BF16)


def terms_kernel(place_ref, count_ref, src_ref, dst_ref, tiles_ref, cot_ref, mine_ref, other_ref, acc_ref):
    live = count_ref[0]
    core = place_ref[1]
    mine_ref[...] = jnp.zeros(mine_ref.shape, BF16)
    other_ref[...] = jnp.zeros(other_ref.shape, BF16)
    for k in range(NT):
        @pl.when(k < live)
        def _():
            acc_ref[src_ref[k]] = jnp.zeros(acc_ref.shape[1:], F32)
    for k in range(NT):
        @pl.when(k < live)
        def _():
            acc_ref[src_ref[k]] += dot(tiles_ref[k], cot_ref[dst_ref[k]], 0, 0)
    for k in range(NT):
        block = src_ref[k]
        member = lax.div(lax.rem(block, 16), 2)
        y = lax.div(member, 2)
        part = lax.rem(block, 2) + 2 * lax.div(block, 16)
        same = lax.rem(member, 2) == core

        @pl.when((k < live) & same)
        def _():
            mine_ref[y, part] = acc_ref[block].astype(BF16)

        @pl.when((k < live) & jnp.logical_not(same))
        def _():
            other_ref[y, part] = acc_ref[block].astype(BF16)


def pair_kernel(place_ref, mine_ref, came_ref, keep_ref, *out_refs):
    y = place_ref[0]
    keep_ref[...] = mine_ref[y].astype(F32) + came_ref[y].astype(F32)
    for step, out_ref in enumerate(out_refs, 1):
        to = lax.rem(y + step, Y)
        out_ref[...] = (mine_ref[to].astype(F32) + came_ref[to].astype(F32)).astype(BF16)


def mid_kernel(keep_ref, came1_ref, came2_ref, came3_ref, features_ref, arrived_ref, own_ref, bound_ref, gw_ref):
    terms = keep_ref[...]
    for came_ref in (came1_ref, came2_ref, came3_ref):
        terms += came_ref[...].astype(F32)
    own = terms[:2].reshape(2 * TILE, -1)
    bound = terms[2:].reshape(2 * TILE, -1)
    own_ref[...] = own
    own_high, own_low = halves(own)
    bound_high, bound_low = halves(bound)
    features = features_ref[...]
    arrived = arrived_ref[...]
    gw = (dot(features, own_high, 0, 0) + dot(features, own_low, 0, 0)
          + dot(arrived, bound_high, 0, 0) + dot(arrived, bound_low, 0, 0))
    for c in range(CHUNKS):
        row, col = c // 2 * 8, c % 2 * 128
        gw_ref[c] = gw[row:row + 8, col:col + 128]
    rows = bound.shape[0]
    x, zl, zh, s = digits(rows, 0, (X, ZL, ZH, SLOTS))
    order = permutation(boundary_row(x, zh, zl, s) == lax.broadcasted_iota(jnp.int32, (rows, rows), 1))
    bound_ref[...] = dot(order, bound_high).astype(BF16)


def pack_kernel(side_ref, near_ref, out_ref):
    rows = side_ref.shape[0]
    zh, x, zl, s = digits(rows, 0, (ZH, X, ZL, SLOTS))
    order = permutation(((x * ZL + zl) * ZH + zh) * SLOTS + s == lax.broadcasted_iota(jnp.int32, (rows, rows), 1))
    lines = rows // ZH
    out_ref[:, :lines, :] = dot(order, side_ref[...]).astype(BF16).reshape(ZH, lines, -1)
    high, low = halves(jnp.sum(near_ref[...], axis=0))
    both = jnp.concatenate([high, low], axis=1)
    for z in range(ZH):
        out_ref[z, lines:, :] = both


def far_kernel(far_ref, done_ref, out_ref):
    del done_ref
    lines = far_ref.shape[1] - 8
    both = jnp.sum(far_ref[:, lines:, :].astype(F32), axis=0)
    out_ref[...] = jnp.broadcast_to((both[:, :128] + both[:, 128:])[None], out_ref.shape)


def back_kernel(idx_ref, own_ref, far_ref, weight_ref, out_ref):
    rows = own_ref.shape[0]
    count = idx_ref.shape[1]
    lines = far_ref.shape[1] - 8
    picks = one_hot(idx_ref, rows)
    zh, x, zl, s = digits(count, 1, (ZH, X, ZL, SLOTS))
    order = permutation(boundary_row(x, zh, zl, s) == lax.broadcasted_iota(jnp.int32, (count, count), 0))
    back = far_ref[:, :lines, :].reshape(count, -1)
    total = own_ref[...] + dot(dot(picks, order).astype(BF16), back)
    high, low = halves(total)
    weight = weight_ref[...]
    out_ref[...] = dot(high, weight, 1, 1) + dot(low, weight, 1, 1)


def forward_kernel(place_ref, count_ref, src_ref, dst_ref, tiles_ref, own_ref, same_ref, twin_ref, weight_ref,
                   out_ref, acc_ref):
    live = count_ref[0]
    acc_ref[...] = jnp.zeros(acc_ref.shape, F32)
    for k in range(NT):
        block = src_ref[k]
        member = lax.div(lax.rem(block, 16), 2)
        away = lax.rem(place_ref[0] - lax.div(member, 2) + Y, Y)
        half = lax.rem(block, 2)
        same = lax.rem(member, 2) == place_ref[1]

        def add(tile, source):
            acc_ref[dst_ref[k]] += dot(tile, source)

        @pl.when((k < live) & (block < 16))
        def _():
            add(tiles_ref[k], own_ref[block])

        @pl.when((k < live) & (block >= 16) & same)
        def _():
            add(tiles_ref[k], same_ref[away, half])

        @pl.when((k < live) & (block >= 16) & jnp.logical_not(same))
        def _():
            add(tiles_ref[k], twin_ref[away, half])
    for t in range(2):
        out_ref[t] = dot(acc_ref[t].astype(BF16), weight_ref[...]).astype(BF16)


def per_device(
    features, tiles, tile_dst, tile_src, tile_count, send_rows, send_count, weight, cotangent
):
    rows, width = features.shape
    groups, slots = send_rows.shape[1:]
    shape = jax.ShapeDtypeStruct
    place = jnp.stack([lax.axis_index("y"), lax.axis_index("core")])
    live = jnp.arange(slots, dtype=jnp.int32)[None, :] < send_count[0][:, None]
    idx = jnp.where(live, send_rows[0], -1).reshape(1, groups * slots)

    outgoing = call(pick_kernel, shape((groups * slots, width), BF16), [VMEM] * 2, "pick")(idx, features)
    arrived = swap(outgoing.reshape(groups, slots, width), GRP).reshape(groups * slots, width)

    part = shape((4, TILE, width), BF16)
    half = shape((Y, 4, TILE, width), BF16)
    mine, other = call(
        terms_kernel, (half, half), [SMEM] * 4 + [VMEM] * 2, "terms", [pltpu.VMEM((32, TILE, width), F32)],
    )(place, tile_count, tile_src, tile_dst, tiles, cotangent.reshape(2, TILE, width))
    came = shift(other, "core", 1, CORE)
    keep, *sent = call(
        pair_kernel, (shape((4, TILE, width), F32), part, part, part), [SMEM] + [VMEM] * 2, "pair",
    )(place, mine, came)
    came = [shift(block, "y", step, Y) for step, block in enumerate(sent, 1)]

    own, bound, gw = call(
        mid_kernel,
        (shape((rows, width), F32), shape((rows, width), BF16), shape((CHUNKS, 8, 128), F32)),
        [VMEM] * 6, "mid",
    )(keep, *came, features, arrived)

    side = swap(bound.reshape(X * ZL, ZH * slots, width), SIDE).reshape(rows, width)
    near = swap(gw, NEAR)
    packed = call(pack_kernel, shape((ZH, rows // ZH + 8, width), BF16), [VMEM] * 2, "pack")(side, near)
    far = swap(packed, FAR)
    all_own = lax.all_gather(features, DEV, axis=0, tiled=True).reshape(16, TILE, width)
    block = arrived.reshape(1, 2, TILE, width)
    same = jnp.concatenate([block] + [shift(block, "y", step, Y) for step in (1, 2, 3)], axis=0)
    twin = shift(same, "core", 1, CORE)
    output = call(
        forward_kernel, shape((2, TILE, width), BF16), [SMEM] * 4 + [VMEM] * 5, "forward",
        [pltpu.VMEM((2, TILE, width), F32)],
    )(place, tile_count, tile_src, tile_dst, tiles, all_own, same, twin, weight)

    spread = call(far_kernel, shape((CHUNKS, 8, 128), F32), [VMEM, ANY], "far")(far, output)
    grad_weight = swap(spread, NEAR).reshape(width // 8, 2, 8, 128).transpose(0, 2, 1, 3).reshape(width, width)
    grad_features = call(back_kernel, shape((rows, width), F32), [VMEM] * 4, "back")(idx, own, far, weight)
    output = output.reshape(rows, width)
    return output, grad_features, grad_weight


def solution(mesh):
    fine = Mesh(mesh.devices.reshape(SIZES), AXES)
    split = [P(AXES)] * 7
    return jax.shard_map(
        per_device,
        mesh=fine,
        in_specs=(*split, P(), P(AXES)),
        out_specs=(P(AXES), P(AXES), P()),
        check_vma=False,
    )
```

```python
import jax
import jax.numpy as jnp
from jax import lax
from jax.experimental import pallas as pl
from jax.experimental.pallas import tpu as pltpu
from jax.sharding import Mesh, PartitionSpec as P

AXES = ("x", "zh", "zl", "y", "core")
SIZES = (4, 16, 2, 4, 2)
SLOTS = 2
X, ZH, ZL, Y, CORE = SIZES
DEV = ("y", "core")
SIDE = ("x", "zl")
NEAR = ("x", "zl", "y", "core")
FAR = "zh"
TILE = 128
NT = 8
CHUNKS = 64

F32 = jnp.float32
BF16 = jnp.bfloat16
SMEM = pl.BlockSpec(memory_space=pltpu.SMEM)
ANY = pl.BlockSpec(memory_space=pl.ANY)
VMEM = pl.BlockSpec(memory_space=pltpu.VMEM)


def swap(x, axes):
    return lax.all_to_all(x, axes, split_axis=0, concat_axis=0, tiled=True)


def shift(x, axis, step, size):
    return lax.ppermute(x, axis, [(i, (i + step) % size) for i in range(size)])


def dot(a, b, da=1, db=0):
    return lax.dot_general(a, b, (((da,), (db,)), ((), ())), preferred_element_type=F32)


def halves(x):
    high = x.astype(BF16)
    return high, (x - high.astype(F32)).astype(BF16)


def call(kernel, out_shape, in_specs, name, scratch=()):
    out_specs = (VMEM,) * len(out_shape) if isinstance(out_shape, tuple) else VMEM
    return pl.pallas_call(
        kernel, out_shape=out_shape, in_specs=in_specs, out_specs=out_specs,
        scratch_shapes=scratch, name=name,
        compiler_params=pltpu.CompilerParams(vmem_limit_bytes=24 * 1024 * 1024),
    )


def digits(count, dim, sizes):
    left = lax.broadcasted_iota(jnp.int32, (count, count), dim)
    found = []
    for size in reversed(sizes):
        found.append(lax.rem(left, size))
        left = lax.div(left, size)
    return found[::-1]


def boundary_row(x, zh, zl, s):
    return ((x * ZH + zh) * ZL + zl) * SLOTS + s


def permutation(match):
    return match.astype(F32).astype(BF16)


def picks(rows, rows_ref, count_ref):
    groups = count_ref.shape[1]
    places = lax.broadcasted_iota(jnp.int32, (rows, groups), 0)
    found = []
    for slot in range(SLOTS):
        live = count_ref[...] > slot
        wanted = jnp.where(live, rows_ref[slot:slot + 1, :], -1)
        found.append(permutation(places == wanted))
    count = groups * SLOTS
    zh, x, zl, s = digits(count, 1, (ZH, X, ZL, SLOTS))
    order = permutation(s * groups + (x * ZH + zh) * ZL + zl == lax.broadcasted_iota(jnp.int32, (count, count), 0))
    return dot(jnp.concatenate(found, axis=1), order).astype(BF16)


def pick_kernel(rows_ref, count_ref, features_ref, out_ref):
    wanted = picks(features_ref.shape[0], rows_ref, count_ref)
    out_ref[...] = dot(wanted, features_ref[...], 0, 0).astype(BF16).reshape(out_ref.shape)


def terms_kernel(place_ref, count_ref, src_ref, dst_ref, tiles_ref, cot_ref, mine_ref, other_ref, acc_ref):
    live = count_ref[0]
    core = place_ref[1]
    mine_ref[...] = jnp.zeros(mine_ref.shape, BF16)
    other_ref[...] = jnp.zeros(other_ref.shape, BF16)
    for k in range(NT):
        @pl.when(k < live)
        def _():
            acc_ref[src_ref[k]] = jnp.zeros(acc_ref.shape[1:], F32)
    for k in range(NT):
        @pl.when(k < live)
        def _():
            acc_ref[src_ref[k]] += dot(tiles_ref[k], cot_ref[dst_ref[k]], 0, 0)
    for k in range(NT):
        block = src_ref[k]
        member = lax.div(lax.rem(block, 16), 2)
        y = lax.div(member, 2)
        part = lax.rem(block, 2) + 2 * lax.div(block, 16)
        same = lax.rem(member, 2) == core

        @pl.when((k < live) & same)
        def _():
            mine_ref[y, part] = acc_ref[block].astype(BF16)

        @pl.when((k < live) & jnp.logical_not(same))
        def _():
            other_ref[y, part] = acc_ref[block].astype(BF16)


def pair_kernel(place_ref, mine_ref, came_ref, keep_ref, *out_refs):
    y = place_ref[0]
    keep_ref[...] = mine_ref[y].astype(F32) + came_ref[y].astype(F32)
    for step, out_ref in enumerate(out_refs, 1):
        to = lax.rem(y + step, Y)
        out_ref[...] = (mine_ref[to].astype(F32) + came_ref[to].astype(F32)).astype(BF16)


def side_kernel(keep_ref, came1_ref, came2_ref, came3_ref, far_ref, done_ref, own_ref, high_ref, low_ref, out_ref):
    del done_ref
    terms = keep_ref[...]
    for came_ref in (came1_ref, came2_ref, came3_ref):
        terms += came_ref[...].astype(F32)
    own_ref[...] = terms[:2].reshape(2 * TILE, -1)
    bound = terms[2:].reshape(2 * TILE, -1)
    rows, width = bound.shape
    column = lax.broadcasted_iota(jnp.int32, (rows, rows), 1)
    x, zl, zh, s = digits(rows, 0, (X, ZL, ZH, SLOTS))
    lines = rows // (X * ZL)
    order = permutation(((zh * X + x) * ZL + zl) * SLOTS + s == column)
    rows_out = dot(order, far_ref[...].reshape(rows, width)).astype(BF16)
    out_ref[:, :lines, :] = rows_out.reshape(X * ZL, lines, width)
    order = permutation(boundary_row(x, zh, zl, s) == column)
    high, low = halves(bound)
    high = dot(order, high).astype(BF16)
    high_ref[...] = high
    low_ref[...] = dot(order, low).astype(BF16)
    out_ref[:, lines:, :] = high.reshape(X * ZL, lines, width)


def mid_kernel(own_ref, high_ref, low_ref, side_ref, features_ref, gw_ref, arrived_ref):
    rows, width = own_ref.shape
    own_high, own_low = halves(own_ref[...])
    features = features_ref[...]
    arrived = side_ref[:, :rows // (X * ZL), :].reshape(rows, width)
    gw = (dot(features, own_high, 0, 0) + dot(features, own_low, 0, 0)
          + dot(arrived, high_ref[...], 0, 0) + dot(arrived, low_ref[...], 0, 0))
    for c in range(CHUNKS):
        row, col = c // 2 * 8, c % 2 * 128
        gw_ref[c] = gw[row:row + 8, col:col + 128]
    x, zl, zh, s = digits(rows, 1, (X, ZL, ZH, SLOTS))
    order = permutation(boundary_row(x, zh, zl, s) == lax.broadcasted_iota(jnp.int32, (rows, rows), 0))
    arrived_ref[...] = dot(order, arrived).astype(BF16)


def pack_kernel(side_ref, near_ref, out_ref):
    lines = out_ref.shape[1] - 8
    rows = ZH * lines
    width = out_ref.shape[2]
    zh, x, zl, s = digits(rows, 0, (ZH, X, ZL, SLOTS))
    order = permutation(((x * ZL + zl) * ZH + zh) * SLOTS + s == lax.broadcasted_iota(jnp.int32, (rows, rows), 1))
    side = side_ref[:, rows // (X * ZL):, :].reshape(rows, width)
    out_ref[:, :lines, :] = dot(order, side).astype(BF16).reshape(ZH, lines, width)
    high, low = halves(jnp.sum(near_ref[...], axis=0))
    both = jnp.concatenate([high, low], axis=1)
    for z in range(ZH):
        out_ref[z, lines:, :] = both


def far_kernel(far_ref, done_ref, out_ref):
    del done_ref
    lines = far_ref.shape[1] - 8
    both = jnp.sum(far_ref[:, lines:, :].astype(F32), axis=0)
    out_ref[...] = jnp.broadcast_to((both[:, :128] + both[:, 128:])[None], out_ref.shape)


def back_kernel(rows_ref, count_ref, own_ref, far_ref, weight_ref, out_ref):
    rows, width = own_ref.shape
    back = far_ref[:, :far_ref.shape[1] - 8, :].reshape(-1, width)
    total = own_ref[...] + dot(picks(rows, rows_ref, count_ref), back)
    high, low = halves(total)
    weight = weight_ref[...]
    out_ref[...] = dot(high, weight, 1, 1) + dot(low, weight, 1, 1)


def forward_kernel(count_ref, src_ref, dst_ref, tiles_ref, own_ref, bound_ref, weight_ref, out_ref, acc_ref):
    live = count_ref[0]
    acc_ref[...] = jnp.zeros(acc_ref.shape, F32)
    for k in range(NT):
        block = src_ref[k]

        @pl.when((k < live) & (block < 16))
        def _():
            acc_ref[dst_ref[k]] += dot(tiles_ref[k], own_ref[block])

        @pl.when((k < live) & (block >= 16))
        def _():
            acc_ref[dst_ref[k]] += dot(tiles_ref[k], bound_ref[block - 16])
    for t in range(2):
        out_ref[t] = dot(acc_ref[t].astype(BF16), weight_ref[...]).astype(BF16)


def per_device(
    features, tiles, tile_dst, tile_src, tile_count, send_rows, send_count, weight, cotangent
):
    rows, width = features.shape
    groups, slots = send_rows.shape[1:]
    lines = groups * slots // ZH
    shape = jax.ShapeDtypeStruct
    place = jnp.stack([lax.axis_index("y"), lax.axis_index("core")])
    send_rows = send_rows.transpose(0, 2, 1).reshape(slots, groups)
    blocked = (16, TILE, width)

    outgoing = call(pick_kernel, shape((ZH, lines, width), BF16), [VMEM] * 3, "pick")(send_rows, send_count, features)
    landed = swap(outgoing, FAR)
    all_own = lax.all_gather(features, DEV, axis=0, tiled=True)

    part = shape((4, TILE, width), BF16)
    half = shape((Y, 4, TILE, width), BF16)
    mine, other = call(
        terms_kernel, (half, half), [SMEM] * 4 + [VMEM] * 2, "terms", [pltpu.VMEM((32, TILE, width), F32)],
    )(place, tile_count, tile_src, tile_dst, tiles, cotangent.reshape(2, TILE, width))
    came = shift(other, "core", 1, CORE)
    keep, *sent = call(
        pair_kernel, (shape((4, TILE, width), F32), part, part, part), [SMEM] + [VMEM] * 2, "pair",
    )(place, mine, came)
    came = [shift(block, "y", step, Y) for step, block in enumerate(sent, 1)]

    square = shape((rows, width), BF16)
    own, high, low, side = call(
        side_kernel,
        (shape((rows, width), F32), square, square, shape((X * ZL, 2 * rows // (X * ZL), width), BF16)),
        [VMEM] * 5 + [ANY], "side",
    )(keep, *came, landed, all_own)
    side = swap(side, SIDE)
    gw, arrived = call(
        mid_kernel, (shape((CHUNKS, 8, 128), F32), square), [VMEM] * 5, "mid",
    )(own, high, low, side, features)
    near = swap(gw, NEAR)
    packed = call(pack_kernel, shape((ZH, lines + 8, width), BF16), [VMEM] * 2, "pack")(side, near)
    far = swap(packed, FAR)

    all_bound = lax.all_gather(arrived, DEV, axis=0, tiled=True)
    output = call(
        forward_kernel, shape((2, TILE, width), BF16), [SMEM] * 3 + [VMEM] * 4, "forward",
        [pltpu.VMEM((2, TILE, width), F32)],
    )(tile_count, tile_src, tile_dst, tiles, all_own.reshape(blocked), all_bound.reshape(blocked), weight)

    spread = call(far_kernel, shape((CHUNKS, 8, 128), F32), [VMEM, ANY], "far")(far, output)
    grad_weight = swap(spread, NEAR).reshape(width // 8, 2, 8, 128).transpose(0, 2, 1, 3).reshape(width, width)
    grad_features = call(back_kernel, shape((rows, width), F32), [VMEM] * 5, "back")(
        send_rows, send_count, own, far, weight)
    return output.reshape(rows, width), grad_features, grad_weight


def solution(mesh):
    fine = Mesh(mesh.devices.reshape(SIZES), AXES)
    split = [P(AXES)] * 7
    return jax.shard_map(
        per_device,
        mesh=fine,
        in_specs=(*split, P(), P(AXES)),
        out_specs=(P(AXES), P(AXES), P()),
        check_vma=False,
    )
```

```python
import jax
import jax.numpy as jnp
from jax import lax
from jax.experimental import pallas as pl
from jax.experimental.pallas import tpu as pltpu
from jax.sharding import Mesh, PartitionSpec as P

AXES = ("x", "zh", "zl", "y", "core")
SIZES = (4, 16, 2, 4, 2)
SLOTS = 2
X, ZH, ZL, Y, CORE = SIZES
DEV = ("y", "core")
SIDE = ("x", "zl")
NEAR = ("x", "zl", "y", "core")
FAR = "zh"
TILE = 128
NT = 8
CHUNKS = 64
SRC = 3
DST = SRC + NT

F32 = jnp.float32
BF16 = jnp.bfloat16
SMEM = pl.BlockSpec(memory_space=pltpu.SMEM)
VMEM = pl.BlockSpec(memory_space=pltpu.VMEM)


def swap(x, axes):
    return lax.all_to_all(x, axes, split_axis=0, concat_axis=0, tiled=True)


def shift(x, axis, step, size):
    return lax.ppermute(x, axis, [(i, (i + step) % size) for i in range(size)])


def dot(a, b, da=1, db=0):
    return lax.dot_general(a, b, (((da,), (db,)), ((), ())), preferred_element_type=F32)


def halves(x):
    high = x.astype(BF16)
    return high, (x - high.astype(F32)).astype(BF16)


def call(kernel, out_shape, in_specs, name, scratch=(), mebibytes=24):
    out_specs = (VMEM,) * len(out_shape) if isinstance(out_shape, tuple) else VMEM
    return pl.pallas_call(
        kernel, out_shape=out_shape, in_specs=in_specs, out_specs=out_specs,
        scratch_shapes=scratch, name=name,
        compiler_params=pltpu.CompilerParams(vmem_limit_bytes=mebibytes * 1024 * 1024),
    )


def digits(count, dim, sizes):
    left = lax.broadcasted_iota(jnp.int32, (count, count), dim)
    found = []
    for size in reversed(sizes):
        found.append(lax.rem(left, size))
        left = lax.div(left, size)
    return found[::-1]


def boundary_row(x, zh, zl, s):
    return ((x * ZH + zh) * ZL + zl) * SLOTS + s


def permutation(match):
    return match.astype(F32).astype(BF16)


def picks(rows, rows_ref, count_ref):
    groups = count_ref.shape[1]
    places = lax.broadcasted_iota(jnp.int32, (rows, groups), 0)
    found = []
    for slot in range(SLOTS):
        live = count_ref[...] > slot
        wanted = jnp.where(live, rows_ref[slot:slot + 1, :], -1)
        found.append(permutation(places == wanted))
    count = groups * SLOTS
    zh, x, zl, s = digits(count, 1, (ZH, X, ZL, SLOTS))
    order = permutation(s * groups + (x * ZH + zh) * ZL + zl == lax.broadcasted_iota(jnp.int32, (count, count), 0))
    return dot(jnp.concatenate(found, axis=1), order).astype(BF16)


def pick_kernel(rows_ref, count_ref, features_ref, out_ref):
    wanted = picks(features_ref.shape[0], rows_ref, count_ref)
    out_ref[...] = dot(wanted, features_ref[...], 0, 0).astype(BF16).reshape(out_ref.shape)


def terms_kernel(meta_ref, tiles_ref, cot_ref, mine_ref, other_ref, acc_ref):
    live, core = meta_ref[0], meta_ref[2]
    mine_ref[...] = jnp.zeros(mine_ref.shape, BF16)
    other_ref[...] = jnp.zeros(other_ref.shape, BF16)
    for k in range(NT):
        @pl.when(k < live)
        def _():
            acc_ref[meta_ref[SRC + k]] = jnp.zeros(acc_ref.shape[1:], F32)
    for k in range(NT):
        @pl.when(k < live)
        def _():
            acc_ref[meta_ref[SRC + k]] += dot(tiles_ref[k], cot_ref[meta_ref[DST + k]], 0, 0)
    for k in range(NT):
        block = meta_ref[SRC + k]
        member = lax.div(lax.rem(block, 16), 2)
        y = lax.div(member, 2)
        part = lax.rem(block, 2) + 2 * lax.div(block, 16)
        same = lax.rem(member, 2) == core

        @pl.when((k < live) & same)
        def _():
            mine_ref[y, part] = acc_ref[block].astype(BF16)

        @pl.when((k < live) & jnp.logical_not(same))
        def _():
            other_ref[y, part] = acc_ref[block].astype(BF16)


def pair_kernel(meta_ref, mine_ref, came_ref, keep_ref, *out_refs):
    y = meta_ref[1]
    keep_ref[...] = mine_ref[y].astype(F32) + came_ref[y].astype(F32)
    for step, out_ref in enumerate(out_refs, 1):
        to = lax.rem(y + step, Y)
        out_ref[...] = (mine_ref[to].astype(F32) + came_ref[to].astype(F32)).astype(BF16)


def side_kernel(keep_ref, came1_ref, came2_ref, came3_ref, far_ref, own_ref, high_ref, low_ref, out_ref):
    terms = keep_ref[...]
    for came_ref in (came1_ref, came2_ref, came3_ref):
        terms += came_ref[...].astype(F32)
    own_ref[...] = terms[:2].reshape(2 * TILE, -1)
    bound = terms[2:].reshape(2 * TILE, -1)
    rows, width = bound.shape
    column = lax.broadcasted_iota(jnp.int32, (rows, rows), 1)
    x, zl, zh, s = digits(rows, 0, (X, ZL, ZH, SLOTS))
    lines = rows // (X * ZL)
    order = permutation(((zh * X + x) * ZL + zl) * SLOTS + s == column)
    rows_out = dot(order, far_ref[...].reshape(rows, width)).astype(BF16)
    out_ref[:, :lines, :] = rows_out.reshape(X * ZL, lines, width)
    order = permutation(boundary_row(x, zh, zl, s) == column)
    high, low = halves(bound)
    high = dot(order, high).astype(BF16)
    high_ref[...] = high
    low_ref[...] = dot(order, low).astype(BF16)
    out_ref[:, lines:, :] = high.reshape(X * ZL, lines, width)


def mid_kernel(own_ref, high_ref, low_ref, side_ref, features_ref, gw_ref, both_ref):
    rows, width = own_ref.shape
    features = features_ref[...]
    arrived = side_ref[:, :rows // (X * ZL), :].reshape(rows, width)
    own_high, own_low = halves(own_ref[...])
    gw = (dot(features, own_high, 0, 0) + dot(features, own_low, 0, 0)
          + dot(arrived, high_ref[...], 0, 0) + dot(arrived, low_ref[...], 0, 0))
    for c in range(CHUNKS):
        row, col = c // 2 * 8, c % 2 * 128
        gw_ref[c] = gw[row:row + 8, col:col + 128]
    x, zl, zh, s = digits(rows, 1, (X, ZL, ZH, SLOTS))
    order = permutation(boundary_row(x, zh, zl, s) == lax.broadcasted_iota(jnp.int32, (rows, rows), 0))
    both_ref[:rows, :] = features
    both_ref[rows:, :] = dot(order, arrived).astype(BF16)


def pack_kernel(side_ref, near_ref, out_ref):
    lines = out_ref.shape[1] // 2 - 4
    rows = ZH * lines
    zh, x, zl, s = digits(rows, 0, (ZH, X, ZL, SLOTS))
    order = permutation(((x * ZL + zl) * ZH + zh) * SLOTS + s == lax.broadcasted_iota(jnp.int32, (rows, rows), 1))
    side = dot(order, side_ref[:, rows // (X * ZL):, :].reshape(rows, -1)).astype(BF16)
    out_ref[:, :lines, :] = side[:, :128].reshape(ZH, lines, 128)
    out_ref[:, lines:2 * lines, :] = side[:, 128:].reshape(ZH, lines, 128)
    near = jnp.sum(near_ref[...], axis=0).astype(BF16)
    for z in range(ZH):
        out_ref[z, 2 * lines:, :] = near


def far_kernel(far_ref, token_ref, out_ref):
    del token_ref
    total = jnp.sum(far_ref[:, far_ref.shape[1] - 8:, :].astype(F32), axis=0)
    out_ref[...] = jnp.broadcast_to(total[None], out_ref.shape)


def back_kernel(rows_ref, count_ref, own_ref, far_ref, weight_ref, out_ref):
    rows = own_ref.shape[0]
    lines = far_ref.shape[1] // 2 - 4
    left = far_ref[:, :lines, :].reshape(ZH * lines, 128)
    right = far_ref[:, lines:2 * lines, :].reshape(ZH * lines, 128)
    total = own_ref[...] + dot(picks(rows, rows_ref, count_ref), jnp.concatenate([left, right], axis=1))
    high, low = halves(total)
    weight = weight_ref[...]
    out_ref[...] = dot(high, weight, 1, 1) + dot(low, weight, 1, 1)


def forward_kernel(meta_ref, tiles_ref, source_ref, weight_ref, out_ref, token_ref, acc_ref):
    live = meta_ref[0]
    token_ref[...] = jnp.zeros(token_ref.shape, F32)
    acc_ref[...] = jnp.zeros(acc_ref.shape, F32)
    for k in range(NT):
        @pl.when(k < live)
        def _():
            block = meta_ref[SRC + k]
            member = lax.div(lax.rem(block, 16), 2)
            part = lax.rem(block, 2) + 2 * lax.div(block, 16)
            acc_ref[meta_ref[DST + k]] += dot(tiles_ref[k], source_ref[member, part])
    for t in range(2):
        out_ref[t] = dot(acc_ref[t].astype(BF16), weight_ref[...]).astype(BF16)


def per_device(
    features, tiles, tile_dst, tile_src, tile_count, send_rows, send_count, weight, cotangent
):
    rows, width = features.shape
    groups, slots = send_rows.shape[1:]
    lines = groups * slots // ZH
    shape = jax.ShapeDtypeStruct
    places = jnp.stack([lax.axis_index("y"), lax.axis_index("core")])
    meta = jnp.concatenate([tile_count, places, tile_src, tile_dst])
    send_rows = send_rows.transpose(0, 2, 1).reshape(slots, groups)

    part = shape((4, TILE, width), BF16)
    half = shape((Y, 4, TILE, width), BF16)
    mine, other = call(
        terms_kernel, (half, half), [SMEM] + [VMEM] * 2, "terms", [pltpu.VMEM((32, TILE, width), F32)], 60,
    )(meta, tiles, cotangent.reshape(2, TILE, width))
    came = shift(other, "core", 1, CORE)
    outgoing = call(pick_kernel, shape((ZH, lines, width), BF16), [VMEM] * 3, "pick", (), 60)(
        send_rows, send_count, features)
    landed = swap(outgoing, FAR)
    keep, *sent = call(
        pair_kernel, (shape((4, TILE, width), F32), part, part, part), [SMEM] + [VMEM] * 2, "pair", (), 60,
    )(meta, mine, came)
    came = [shift(block, "y", step, Y) for step, block in enumerate(sent, 1)]

    square = shape((rows, width), BF16)
    own, high, low, side = call(
        side_kernel,
        (shape((rows, width), F32), square, square, shape((X * ZL, 2 * rows // (X * ZL), width), BF16)),
        [VMEM] * 5, "side",
    )(keep, *came, landed)
    side = swap(side, SIDE)
    gw, both = call(
        mid_kernel, (shape((CHUNKS, 8, 128), F32), shape((2 * rows, width), BF16)), [VMEM] * 5, "mid",
    )(own, high, low, side, features)
    near = swap(gw, NEAR)
    packed = call(pack_kernel, shape((ZH, 2 * lines + 8, 128), BF16), [VMEM] * 2, "pack")(side, near)
    far = swap(packed, FAR)

    source = lax.all_gather(both, DEV, axis=0, tiled=True).reshape(Y * CORE, 4, TILE, width)
    output, token = call(
        forward_kernel, (shape((2, TILE, width), BF16), shape((8, 128), F32)), [SMEM] + [VMEM] * 3, "forward",
        [pltpu.VMEM((2, TILE, width), F32)],
    )(meta, tiles, source, weight)

    spread = call(far_kernel, shape((CHUNKS, 8, 128), F32), [VMEM] * 2, "far")(far, token)
    grad_weight = swap(spread, NEAR).reshape(width // 8, 2, 8, 128).transpose(0, 2, 1, 3).reshape(width, width)
    grad_features = call(back_kernel, shape((rows, width), F32), [VMEM] * 5, "back")(
        send_rows, send_count, own, far, weight)
    return output.reshape(rows, width), grad_features, grad_weight


def solution(mesh):
    fine = Mesh(mesh.devices.reshape(SIZES), AXES)
    split = [P(AXES)] * 7
    return jax.shard_map(
        per_device,
        mesh=fine,
        in_specs=(*split, P(), P(AXES)),
        out_specs=(P(AXES), P(AXES), P()),
        check_vma=False,
    )
```

```python
import functools

import jax
import jax.numpy as jnp
from jax import lax
from jax.experimental import pallas as pl
from jax.experimental.pallas import tpu as pltpu
from jax.sharding import Mesh, PartitionSpec as P

AXES = ("x", "zh", "zl", "y", "core")
SIZES = (4, 16, 2, 4, 2)
SLOTS = 2
X, ZH, ZL, Y, CORE = SIZES
DEV = ("y", "core")
SIDE = ("x", "zl")
NEAR = ("x", "zl", "y", "core")
FAR = "zh"
TILE = 128
NT = 8
PAIR = 24
CHUNKS = 64
SRC = 3
DST = SRC + NT

F32 = jnp.float32
BF16 = jnp.bfloat16
SMEM = pl.BlockSpec(memory_space=pltpu.SMEM)
ANY = pl.BlockSpec(memory_space=pl.ANY)
VMEM = pl.BlockSpec(memory_space=pltpu.VMEM)


def swap(x, axes):
    return lax.all_to_all(x, axes, split_axis=0, concat_axis=0, tiled=True)


def shift(x, axis, step, size):
    return lax.ppermute(x, axis, [(i, (i + step) % size) for i in range(size)])


def dot(a, b, da=1, db=0):
    return lax.dot_general(a, b, (((da,), (db,)), ((), ())), preferred_element_type=F32)


def halves(x):
    high = x.astype(BF16)
    return high, (x - high.astype(F32)).astype(BF16)


def call(kernel, out_shape, in_specs, name, scratch=(), mebibytes=24):
    out_specs = (VMEM,) * len(out_shape) if isinstance(out_shape, tuple) else VMEM
    return pl.pallas_call(
        kernel, out_shape=out_shape, in_specs=in_specs, out_specs=out_specs,
        scratch_shapes=scratch, name=name,
        compiler_params=pltpu.CompilerParams(vmem_limit_bytes=mebibytes * 1024 * 1024),
    )


def digits(count, dim, sizes):
    left = lax.broadcasted_iota(jnp.int32, (count, count), dim)
    found = []
    for size in reversed(sizes):
        found.append(lax.rem(left, size))
        left = lax.div(left, size)
    return found[::-1]


def boundary_row(x, zh, zl, s):
    return ((x * ZH + zh) * ZL + zl) * SLOTS + s


def permutation(match):
    return match.astype(F32).astype(BF16)


def picks(rows, rows_ref, count_ref):
    groups = count_ref.shape[1]
    places = lax.broadcasted_iota(jnp.int32, (rows, groups), 0)
    found = []
    for slot in range(SLOTS):
        live = count_ref[...] > slot
        wanted = jnp.where(live, rows_ref[slot:slot + 1, :], -1)
        found.append(permutation(places == wanted))
    count = groups * SLOTS
    zh, x, zl, s = digits(count, 1, (ZH, X, ZL, SLOTS))
    order = permutation(s * groups + (x * ZH + zh) * ZL + zl == lax.broadcasted_iota(jnp.int32, (count, count), 0))
    return dot(jnp.concatenate(found, axis=1), order).astype(BF16)


def pick_kernel(rows_ref, count_ref, features_ref, out_ref):
    wanted = picks(features_ref.shape[0], rows_ref, count_ref)
    out_ref[...] = dot(wanted, features_ref[...], 0, 0).astype(BF16).reshape(out_ref.shape)


def terms_kernel(meta_ref, tiles_ref, cot_ref, mine_ref, other_ref, acc_ref):
    live, core = meta_ref[0], meta_ref[2]
    mine_ref[...] = jnp.zeros(mine_ref.shape, BF16)
    other_ref[...] = jnp.zeros(other_ref.shape, BF16)
    for k in range(NT):
        @pl.when(k < live)
        def _():
            acc_ref[meta_ref[SRC + k]] = jnp.zeros(acc_ref.shape[1:], F32)
    for k in range(NT):
        @pl.when(k < live)
        def _():
            acc_ref[meta_ref[SRC + k]] += dot(tiles_ref[k], cot_ref[meta_ref[DST + k]], 0, 0)
    for k in range(NT):
        block = meta_ref[SRC + k]
        member = lax.div(lax.rem(block, 16), 2)
        y = lax.div(member, 2)
        kind, part = lax.div(block, 16), lax.rem(block, 2)
        same = lax.rem(member, 2) == core

        @pl.when((k < live) & same)
        def _():
            mine_ref[kind, y, part] = acc_ref[block].astype(BF16)

        @pl.when((k < live) & jnp.logical_not(same))
        def _():
            other_ref[kind, y, part] = acc_ref[block].astype(BF16)


def pair_kernel(kind, meta_ref, mine_in, came_in, *rest):
    keep_ref, *out_refs, mine_ref, came_ref, sems = rest[-7:]
    copies = [pltpu.make_async_copy(mine_in.at[kind], mine_ref, sems.at[0]),
              pltpu.make_async_copy(came_in.at[kind], came_ref, sems.at[1])]
    for copy in copies:
        copy.start()
    for copy in copies:
        copy.wait()
    y = meta_ref[1]
    keep_ref[...] = mine_ref[y].astype(F32) + came_ref[y].astype(F32)
    for step, out_ref in enumerate(out_refs, 1):
        to = lax.rem(y + step, Y)
        out_ref[...] = (mine_ref[to].astype(F32) + came_ref[to].astype(F32)).astype(BF16)


def sum_kernel(keep_ref, came1_ref, came2_ref, came3_ref, token_ref, out_ref, out_token_ref):
    out_token_ref[...] = token_ref[...]
    terms = keep_ref[...]
    for came_ref in (came1_ref, came2_ref, came3_ref):
        terms += came_ref[...].astype(F32)
    out_ref[...] = terms.reshape(out_ref.shape)


def own_kernel(meta_ref, tiles_ref, cot_ref, source_ref, out_ref):
    live = meta_ref[0]
    out_ref[...] = jnp.zeros(out_ref.shape, F32)
    for k in range(NT):
        block = meta_ref[SRC + k]

        @pl.when((k < live) & (block < 16))
        def _():
            high, low = halves(dot(tiles_ref[k], cot_ref[meta_ref[DST + k]], 0, 0))
            source = source_ref[block]
            out_ref[...] += dot(source, high, 0, 0) + dot(source, low, 0, 0)


def side_kernel(keep_ref, came1_ref, came2_ref, came3_ref, far_ref, own_ref, high_ref, low_ref, out_ref):
    del own_ref
    terms = keep_ref[...]
    for came_ref in (came1_ref, came2_ref, came3_ref):
        terms += came_ref[...].astype(F32)
    bound = terms.reshape(2 * TILE, -1)
    rows, width = bound.shape
    column = lax.broadcasted_iota(jnp.int32, (rows, rows), 1)
    x, zl, zh, s = digits(rows, 0, (X, ZL, ZH, SLOTS))
    lines = rows // (X * ZL)
    order = permutation(((zh * X + x) * ZL + zl) * SLOTS + s == column)
    rows_out = dot(order, far_ref[...].reshape(rows, width)).astype(BF16)
    out_ref[:, :lines, :] = rows_out.reshape(X * ZL, lines, width)
    order = permutation(boundary_row(x, zh, zl, s) == column)
    high, low = halves(bound)
    high = dot(order, high).astype(BF16)
    high_ref[...] = high
    low_ref[...] = dot(order, low).astype(BF16)
    out_ref[:, lines:, :] = high.reshape(X * ZL, lines, width)


def mid_kernel(own_ref, high_ref, low_ref, side_ref, gw_ref, arrived_ref):
    rows, width = high_ref.shape
    arrived = side_ref[:, :rows // (X * ZL), :].reshape(rows, width)
    gw = own_ref[...] + dot(arrived, high_ref[...], 0, 0) + dot(arrived, low_ref[...], 0, 0)
    for c in range(CHUNKS):
        row, col = c // 2 * 8, c % 2 * 128
        gw_ref[c] = gw[row:row + 8, col:col + 128]
    x, zl, zh, s = digits(rows, 1, (X, ZL, ZH, SLOTS))
    order = permutation(boundary_row(x, zh, zl, s) == lax.broadcasted_iota(jnp.int32, (rows, rows), 0))
    arrived_ref[...] = dot(order, arrived).astype(BF16)


def pack_kernel(side_ref, near_ref, out_ref, token_ref):
    token_ref[...] = jnp.zeros(token_ref.shape, F32)
    lines = out_ref.shape[1] // 2 - 4
    rows = ZH * lines
    zh, x, zl, s = digits(rows, 0, (ZH, X, ZL, SLOTS))
    order = permutation(((x * ZL + zl) * ZH + zh) * SLOTS + s == lax.broadcasted_iota(jnp.int32, (rows, rows), 1))
    side = dot(order, side_ref[:, rows // (X * ZL):, :].reshape(rows, -1)).astype(BF16)
    out_ref[:, :lines, :] = side[:, :128].reshape(ZH, lines, 128)
    out_ref[:, lines:2 * lines, :] = side[:, 128:].reshape(ZH, lines, 128)
    near = jnp.sum(near_ref[...], axis=0).astype(BF16)
    for z in range(ZH):
        out_ref[z, 2 * lines:, :] = near


def far_kernel(far_ref, token_ref, out_ref):
    del token_ref
    total = jnp.sum(far_ref[:, far_ref.shape[1] - 8:, :].astype(F32), axis=0)
    out_ref[...] = jnp.broadcast_to(total[None], out_ref.shape)


def back_kernel(rows_ref, count_ref, own_ref, far_ref, weight_ref, out_ref):
    rows = own_ref.shape[0]
    lines = far_ref.shape[1] // 2 - 4
    left = far_ref[:, :lines, :].reshape(ZH * lines, 128)
    right = far_ref[:, lines:2 * lines, :].reshape(ZH * lines, 128)
    total = own_ref[...] + dot(picks(rows, rows_ref, count_ref), jnp.concatenate([left, right], axis=1))
    high, low = halves(total)
    weight = weight_ref[...]
    out_ref[...] = dot(high, weight, 1, 1) + dot(low, weight, 1, 1)


def forward_kernel(meta_ref, tiles_ref, own_ref, bound_ref, weight_ref, out_ref, token_ref, acc_ref):
    live = meta_ref[0]
    token_ref[...] = jnp.zeros(token_ref.shape, F32)
    acc_ref[...] = jnp.zeros(acc_ref.shape, F32)
    for k in range(NT):
        block = meta_ref[SRC + k]

        @pl.when((k < live) & (block < 16))
        def _():
            acc_ref[meta_ref[DST + k]] += dot(tiles_ref[k], own_ref[block])

        @pl.when((k < live) & (block >= 16))
        def _():
            acc_ref[meta_ref[DST + k]] += dot(tiles_ref[k], bound_ref[block - 16])
    for t in range(2):
        out_ref[t] = dot(acc_ref[t].astype(BF16), weight_ref[...]).astype(BF16)


def per_device(
    features, tiles, tile_dst, tile_src, tile_count, send_rows, send_count, weight, cotangent
):
    rows, width = features.shape
    groups, slots = send_rows.shape[1:]
    lines = groups * slots // ZH
    shape = jax.ShapeDtypeStruct
    places = jnp.stack([lax.axis_index("y"), lax.axis_index("core")])
    meta = jnp.concatenate([tile_count, places, tile_src, tile_dst])
    send_rows = send_rows.transpose(0, 2, 1).reshape(slots, groups)

    cotangent = cotangent.reshape(2, TILE, width)
    blocked = (16, TILE, width)
    square = shape((rows, width), BF16)
    token = shape((8, 128), F32)

    all_own = lax.all_gather(features, DEV, axis=0, tiled=True).reshape(blocked)

    half = shape((2, Y, 2, TILE, width), BF16)
    mine, other = call(
        terms_kernel, (half, half), [SMEM] + [VMEM] * 2, "terms", [pltpu.VMEM((32, TILE, width), F32)], 60,
    )(meta, tiles, cotangent)
    came = shift(other, "core", 1, CORE)
    outgoing = call(pick_kernel, shape((ZH, lines, width), BF16), [VMEM] * 3, "pick", (), 60)(
        send_rows, send_count, features)
    landed = swap(outgoing, FAR)

    def exchange(kind, name, after):
        held = pltpu.VMEM((Y, 2, TILE, width), BF16)
        part = shape((2, TILE, width), BF16)
        keep, *sent = call(
            functools.partial(pair_kernel, kind), (shape(part.shape, F32), part, part, part), [SMEM, ANY, ANY] + [VMEM] * len(after),
            name, [held, held, pltpu.SemaphoreType.DMA((2,))], PAIR,
        )(meta, mine, came, *after)
        return keep, [shift(block, "y", step, Y) for step, block in enumerate(sent, 1)]

    keep, sums = exchange(1, "pair_bound", ())
    gw_own = call(own_kernel, shape((width, width), F32), [SMEM] + [VMEM] * 3, "own")(meta, tiles, cotangent, all_own)
    high, low, side = call(
        side_kernel, (square, square, shape((X * ZL, 2 * rows // (X * ZL), width), BF16)), [VMEM] * 5 + [ANY], "side",
    )(keep, *sums, landed, gw_own)
    side = swap(side, SIDE)
    gw, arrived = call(
        mid_kernel, (shape((CHUNKS, 8, 128), F32), square), [VMEM] * 4, "mid",
    )(gw_own, high, low, side)
    near = swap(gw, NEAR)
    packed, packed_token = call(
        pack_kernel, (shape((ZH, 2 * lines + 8, 128), BF16), token), [VMEM] * 2, "pack",
    )(side, near)
    far = swap(packed, FAR)

    all_bound = lax.all_gather(arrived, DEV, axis=0, tiled=True).reshape(blocked)
    output, forward_token = call(
        forward_kernel, (shape((2, TILE, width), BF16), token), [SMEM] + [VMEM] * 4, "forward",
        [pltpu.VMEM((2, TILE, width), F32)],
    )(meta, tiles, all_own, all_bound, weight)
    keep, sums = exchange(0, "pair_own", (packed_token,))
    own, last_token = call(sum_kernel, (shape((rows, width), F32), token), [VMEM] * 5, "sum")(
        keep, *sums, forward_token)

    spread = call(far_kernel, shape((CHUNKS, 8, 128), F32), [VMEM] * 2, "far")(far, last_token)
    grad_weight = swap(spread, NEAR).reshape(width // 8, 2, 8, 128).transpose(0, 2, 1, 3).reshape(width, width)
    grad_features = call(back_kernel, shape((rows, width), F32), [VMEM] * 5, "back")(
        send_rows, send_count, own, far, weight)
    return output.reshape(rows, width), grad_features, grad_weight


def solution(mesh):
    fine = Mesh(mesh.devices.reshape(SIZES), AXES)
    split = [P(AXES)] * 7
    return jax.shard_map(
        per_device,
        mesh=fine,
        in_specs=(*split, P(), P(AXES)),
        out_specs=(P(AXES), P(AXES), P()),
        check_vma=False,
    )
```

```python
import functools

import jax
import jax.numpy as jnp
from jax import lax
from jax.experimental import pallas as pl
from jax.experimental.pallas import tpu as pltpu
from jax.sharding import Mesh, PartitionSpec as P

AXES = ("x", "zh", "zl", "y", "core")
SIZES = (4, 16, 2, 4, 2)
SLOTS = 2
X, ZH, ZL, Y, CORE = SIZES
DEV = ("y", "core")
SIDE = ("x", "zl")
NEAR = ("x", "zl", "y", "core")
FAR = "zh"
TILE = 128
NT = 8
CHUNKS = 64
SRC = 3
DST = SRC + NT

F32 = jnp.float32
BF16 = jnp.bfloat16
SMEM = pl.BlockSpec(memory_space=pltpu.SMEM)
ANY = pl.BlockSpec(memory_space=pl.ANY)
VMEM = pl.BlockSpec(memory_space=pltpu.VMEM)


def swap(x, axes):
    return lax.all_to_all(x, axes, split_axis=0, concat_axis=0, tiled=True)


def shift(x, axis, step, size):
    return lax.ppermute(x, axis, [(i, (i + step) % size) for i in range(size)])


def dot(a, b, da=1, db=0):
    return lax.dot_general(a, b, (((da,), (db,)), ((), ())), preferred_element_type=F32)


def halves(x):
    high = x.astype(BF16)
    return high, (x - high.astype(F32)).astype(BF16)


def call(kernel, out_shape, in_specs, name, scratch=(), mebibytes=24):
    out_specs = (VMEM,) * len(out_shape) if isinstance(out_shape, tuple) else VMEM
    return pl.pallas_call(
        kernel, out_shape=out_shape, in_specs=in_specs, out_specs=out_specs,
        scratch_shapes=scratch, name=name,
        compiler_params=pltpu.CompilerParams(vmem_limit_bytes=mebibytes * 1024 * 1024),
    )


def digits(count, dim, sizes):
    left = lax.broadcasted_iota(jnp.int32, (count, count), dim)
    found = []
    for size in reversed(sizes):
        found.append(lax.rem(left, size))
        left = lax.div(left, size)
    return found[::-1]


def boundary_row(x, zh, zl, s):
    return ((x * ZH + zh) * ZL + zl) * SLOTS + s


def permutation(match):
    return match.astype(F32).astype(BF16)


def picks(rows, rows_ref, count_ref):
    groups = count_ref.shape[1]
    places = lax.broadcasted_iota(jnp.int32, (rows, groups), 0)
    found = []
    for slot in range(SLOTS):
        live = count_ref[...] > slot
        wanted = jnp.where(live, rows_ref[slot:slot + 1, :], -1)
        found.append(permutation(places == wanted))
    count = groups * SLOTS
    zh, x, zl, s = digits(count, 1, (ZH, X, ZL, SLOTS))
    order = permutation(s * groups + (x * ZH + zh) * ZL + zl == lax.broadcasted_iota(jnp.int32, (count, count), 0))
    return dot(jnp.concatenate(found, axis=1), order).astype(BF16)


def pick_kernel(rows_ref, count_ref, features_ref, out_ref):
    wanted = picks(features_ref.shape[0], rows_ref, count_ref)
    out_ref[...] = dot(wanted, features_ref[...], 0, 0).astype(BF16).reshape(out_ref.shape)


def terms_kernel(kind, meta_ref, tiles_ref, cot_ref, token_ref, mine_ref, other_ref, acc_ref):
    del token_ref
    live, core = meta_ref[0], meta_ref[2]
    mine_ref[...] = jnp.zeros(mine_ref.shape, BF16)
    other_ref[...] = jnp.zeros(other_ref.shape, BF16)

    def each(k, act):
        block = meta_ref[SRC + k]
        pl.when((k < live) & (lax.div(block, 16) == kind))(lambda: act(lax.rem(block, 16)))

    for k in range(NT):
        @functools.partial(each, k)
        def _(block):
            acc_ref[block] = jnp.zeros(acc_ref.shape[1:], F32)
    for k in range(NT):
        @functools.partial(each, k)
        def _(block):
            acc_ref[block] += dot(tiles_ref[k], cot_ref[meta_ref[DST + k]], 0, 0)
    for k in range(NT):
        @functools.partial(each, k)
        def _(block):
            member, part = lax.div(block, 2), lax.rem(block, 2)
            y, same = lax.div(member, 2), lax.rem(member, 2) == core

            @pl.when(same)
            def _():
                mine_ref[y, part] = acc_ref[block].astype(BF16)

            @pl.when(jnp.logical_not(same))
            def _():
                other_ref[y, part] = acc_ref[block].astype(BF16)


def pair_kernel(meta_ref, mine_ref, came_ref, keep_ref, *out_refs):
    y = meta_ref[1]
    keep_ref[...] = mine_ref[y].astype(F32) + came_ref[y].astype(F32)
    for step, out_ref in enumerate(out_refs, 1):
        to = lax.rem(y + step, Y)
        out_ref[...] = (mine_ref[to].astype(F32) + came_ref[to].astype(F32)).astype(BF16)


def sum_kernel(keep_ref, came1_ref, came2_ref, came3_ref, token_ref, out_ref, out_token_ref):
    out_token_ref[...] = token_ref[...]
    terms = keep_ref[...]
    for came_ref in (came1_ref, came2_ref, came3_ref):
        terms += came_ref[...].astype(F32)
    out_ref[...] = terms.reshape(out_ref.shape)


def own_kernel(meta_ref, tiles_ref, cot_ref, source_ref, out_ref):
    live = meta_ref[0]
    out_ref[...] = jnp.zeros(out_ref.shape, F32)
    for k in range(NT):
        block = meta_ref[SRC + k]

        @pl.when((k < live) & (block < 16))
        def _():
            high, low = halves(dot(tiles_ref[k], cot_ref[meta_ref[DST + k]], 0, 0))
            source = source_ref[block]
            out_ref[...] += dot(source, high, 0, 0) + dot(source, low, 0, 0)


def side_kernel(keep_ref, came1_ref, came2_ref, came3_ref, far_ref, own_ref, high_ref, low_ref, out_ref):
    del own_ref
    terms = keep_ref[...]
    for came_ref in (came1_ref, came2_ref, came3_ref):
        terms += came_ref[...].astype(F32)
    bound = terms.reshape(2 * TILE, -1)
    rows, width = bound.shape
    column = lax.broadcasted_iota(jnp.int32, (rows, rows), 1)
    x, zl, zh, s = digits(rows, 0, (X, ZL, ZH, SLOTS))
    lines = rows // (X * ZL)
    order = permutation(((zh * X + x) * ZL + zl) * SLOTS + s == column)
    rows_out = dot(order, far_ref[...].reshape(rows, width)).astype(BF16)
    out_ref[:, :lines, :] = rows_out.reshape(X * ZL, lines, width)
    order = permutation(boundary_row(x, zh, zl, s) == column)
    high, low = halves(bound)
    high = dot(order, high).astype(BF16)
    high_ref[...] = high
    low_ref[...] = dot(order, low).astype(BF16)
    out_ref[:, lines:, :] = high.reshape(X * ZL, lines, width)


def mid_kernel(own_ref, high_ref, low_ref, side_ref, gw_ref, arrived_ref, token_ref):
    token_ref[...] = jnp.zeros(token_ref.shape, F32)
    rows, width = high_ref.shape
    arrived = side_ref[:, :rows // (X * ZL), :].reshape(rows, width)
    gw = own_ref[...] + dot(arrived, high_ref[...], 0, 0) + dot(arrived, low_ref[...], 0, 0)
    for c in range(CHUNKS):
        row, col = c // 2 * 8, c % 2 * 128
        gw_ref[c] = gw[row:row + 8, col:col + 128]
    x, zl, zh, s = digits(rows, 1, (X, ZL, ZH, SLOTS))
    order = permutation(boundary_row(x, zh, zl, s) == lax.broadcasted_iota(jnp.int32, (rows, rows), 0))
    arrived_ref[...] = dot(order, arrived).astype(BF16)


def pack_kernel(side_ref, near_ref, out_ref):
    lines = out_ref.shape[1] // 2 - 4
    rows = ZH * lines
    zh, x, zl, s = digits(rows, 0, (ZH, X, ZL, SLOTS))
    order = permutation(((x * ZL + zl) * ZH + zh) * SLOTS + s == lax.broadcasted_iota(jnp.int32, (rows, rows), 1))
    side = dot(order, side_ref[:, rows // (X * ZL):, :].reshape(rows, -1)).astype(BF16)
    out_ref[:, :lines, :] = side[:, :128].reshape(ZH, lines, 128)
    out_ref[:, lines:2 * lines, :] = side[:, 128:].reshape(ZH, lines, 128)
    near = jnp.sum(near_ref[...], axis=0).astype(BF16)
    for z in range(ZH):
        out_ref[z, 2 * lines:, :] = near


def far_kernel(far_ref, token_ref, out_ref):
    del token_ref
    total = jnp.sum(far_ref[:, far_ref.shape[1] - 8:, :].astype(F32), axis=0)
    out_ref[...] = jnp.broadcast_to(total[None], out_ref.shape)


def back_kernel(rows_ref, count_ref, own_ref, far_ref, weight_ref, out_ref):
    rows = own_ref.shape[0]
    lines = far_ref.shape[1] // 2 - 4
    left = far_ref[:, :lines, :].reshape(ZH * lines, 128)
    right = far_ref[:, lines:2 * lines, :].reshape(ZH * lines, 128)
    total = own_ref[...] + dot(picks(rows, rows_ref, count_ref), jnp.concatenate([left, right], axis=1))
    high, low = halves(total)
    weight = weight_ref[...]
    out_ref[...] = dot(high, weight, 1, 1) + dot(low, weight, 1, 1)


def forward_kernel(meta_ref, tiles_ref, own_ref, bound_ref, weight_ref, out_ref, token_ref, acc_ref):
    live = meta_ref[0]
    token_ref[...] = jnp.zeros(token_ref.shape, F32)
    acc_ref[...] = jnp.zeros(acc_ref.shape, F32)
    for k in range(NT):
        block = meta_ref[SRC + k]

        @pl.when((k < live) & (block < 16))
        def _():
            acc_ref[meta_ref[DST + k]] += dot(tiles_ref[k], own_ref[block])

        @pl.when((k < live) & (block >= 16))
        def _():
            acc_ref[meta_ref[DST + k]] += dot(tiles_ref[k], bound_ref[block - 16])
    for t in range(2):
        out_ref[t] = dot(acc_ref[t].astype(BF16), weight_ref[...]).astype(BF16)


def per_device(
    features, tiles, tile_dst, tile_src, tile_count, send_rows, send_count, weight, cotangent
):
    rows, width = features.shape
    groups, slots = send_rows.shape[1:]
    lines = groups * slots // ZH
    shape = jax.ShapeDtypeStruct
    places = jnp.stack([lax.axis_index("y"), lax.axis_index("core")])
    meta = jnp.concatenate([tile_count, places, tile_src, tile_dst])
    send_rows = send_rows.transpose(0, 2, 1).reshape(slots, groups)

    cotangent = cotangent.reshape(2, TILE, width)
    blocked = (16, TILE, width)
    square = shape((rows, width), BF16)
    token = shape((8, 128), F32)

    all_own = lax.all_gather(features, DEV, axis=0, tiled=True).reshape(blocked)

    outgoing = call(pick_kernel, shape((ZH, lines, width), BF16), [VMEM] * 3, "pick", (), 60)(
        send_rows, send_count, features)
    landed = swap(outgoing, FAR)

    def exchange(kind, name, after):
        half = shape((Y, 2, TILE, width), BF16)
        part = shape((2, TILE, width), BF16)
        mine, other = call(
            functools.partial(terms_kernel, kind), (half, half), [SMEM, VMEM, VMEM, ANY], "terms_" + name,
            [pltpu.VMEM((16, TILE, width), F32)],
        )(meta, tiles, cotangent, after)
        came = shift(other, "core", 1, CORE)
        keep, *sent = call(
            pair_kernel, (shape(part.shape, F32), part, part, part), [SMEM] + [VMEM] * 2, "pair_" + name,
        )(meta, mine, came)
        return keep, [shift(block, "y", step, Y) for step, block in enumerate(sent, 1)]

    keep, sums = exchange(1, "bound", outgoing)
    gw_own = call(own_kernel, shape((width, width), F32), [SMEM] + [VMEM] * 3, "own")(meta, tiles, cotangent, all_own)
    high, low, side = call(
        side_kernel, (square, square, shape((X * ZL, 2 * rows // (X * ZL), width), BF16)), [VMEM] * 5 + [ANY], "side",
    )(keep, *sums, landed, gw_own)
    side = swap(side, SIDE)
    gw, arrived, mid_token = call(
        mid_kernel, (shape((CHUNKS, 8, 128), F32), square, token), [VMEM] * 4, "mid",
    )(gw_own, high, low, side)
    near = swap(gw, NEAR)
    packed = call(pack_kernel, shape((ZH, 2 * lines + 8, 128), BF16), [VMEM] * 2, "pack")(side, near)
    far = swap(packed, FAR)

    all_bound = lax.all_gather(arrived, DEV, axis=0, tiled=True).reshape(blocked)
    output, forward_token = call(
        forward_kernel, (shape((2, TILE, width), BF16), token), [SMEM] + [VMEM] * 4, "forward",
        [pltpu.VMEM((2, TILE, width), F32)],
    )(meta, tiles, all_own, all_bound, weight)
    keep, sums = exchange(0, "own", mid_token)
    own, last_token = call(sum_kernel, (shape((rows, width), F32), token), [VMEM] * 5, "sum")(
        keep, *sums, forward_token)

    spread = call(far_kernel, shape((CHUNKS, 8, 128), F32), [VMEM] * 2, "far")(far, last_token)
    grad_weight = swap(spread, NEAR).reshape(width // 8, 2, 8, 128).transpose(0, 2, 1, 3).reshape(width, width)
    grad_features = call(back_kernel, shape((rows, width), F32), [VMEM] * 5, "back")(
        send_rows, send_count, own, far, weight)
    return output.reshape(rows, width), grad_features, grad_weight


def solution(mesh):
    fine = Mesh(mesh.devices.reshape(SIZES), AXES)
    split = [P(AXES)] * 7
    return jax.shard_map(
        per_device,
        mesh=fine,
        in_specs=(*split, P(), P(AXES)),
        out_specs=(P(AXES), P(AXES), P()),
        check_vma=False,
    )
```

```python
import functools

import jax
import jax.numpy as jnp
from jax import lax
from jax.experimental import pallas as pl
from jax.experimental.pallas import tpu as pltpu
from jax.sharding import Mesh, PartitionSpec as P

AXES = ("x", "zh", "zl", "y", "core")
SIZES = (4, 16, 2, 4, 2)
SLOTS = 2
X, ZH, ZL, Y, CORE = SIZES
DEV = ("y", "core")
SIDE = ("x", "zl")
NEAR = ("x", "zl", "y", "core")
FAR = "zh"
TILE = 128
NT = 8
CHUNKS = 64
SRC = 3
DST = SRC + NT

F32 = jnp.float32
BF16 = jnp.bfloat16
SMEM = pl.BlockSpec(memory_space=pltpu.SMEM)
ANY = pl.BlockSpec(memory_space=pl.ANY)
VMEM = pl.BlockSpec(memory_space=pltpu.VMEM)


def swap(x, axes):
    return lax.all_to_all(x, axes, split_axis=0, concat_axis=0, tiled=True)


def shift(x, axis, step, size):
    return lax.ppermute(x, axis, [(i, (i + step) % size) for i in range(size)])


def dot(a, b, da=1, db=0):
    return lax.dot_general(a, b, (((da,), (db,)), ((), ())), preferred_element_type=F32)


def halves(x):
    high = x.astype(BF16)
    return high, (x - high.astype(F32)).astype(BF16)


def call(kernel, out_shape, in_specs, name, scratch=(), mebibytes=24):
    out_specs = (VMEM,) * len(out_shape) if isinstance(out_shape, tuple) else VMEM
    return pl.pallas_call(
        kernel, out_shape=out_shape, in_specs=in_specs, out_specs=out_specs,
        scratch_shapes=scratch, name=name,
        compiler_params=pltpu.CompilerParams(vmem_limit_bytes=mebibytes * 1024 * 1024),
    )


def digits(count, dim, sizes):
    left = lax.broadcasted_iota(jnp.int32, (count, count), dim)
    found = []
    for size in reversed(sizes):
        found.append(lax.rem(left, size))
        left = lax.div(left, size)
    return found[::-1]


def boundary_row(x, zh, zl, s):
    return ((x * ZH + zh) * ZL + zl) * SLOTS + s


def permutation(match):
    return match.astype(F32).astype(BF16)


def picks(rows, rows_ref, count_ref):
    groups = count_ref.shape[1]
    places = lax.broadcasted_iota(jnp.int32, (rows, groups), 0)
    found = []
    for slot in range(SLOTS):
        live = count_ref[...] > slot
        wanted = jnp.where(live, rows_ref[slot:slot + 1, :], -1)
        found.append(permutation(places == wanted))
    count = groups * SLOTS
    zh, x, zl, s = digits(count, 1, (ZH, X, ZL, SLOTS))
    order = permutation(s * groups + (x * ZH + zh) * ZL + zl == lax.broadcasted_iota(jnp.int32, (count, count), 0))
    return dot(jnp.concatenate(found, axis=1), order).astype(BF16)


def pick_kernel(rows_ref, count_ref, features_ref, out_ref):
    wanted = picks(features_ref.shape[0], rows_ref, count_ref)
    out_ref[...] = dot(wanted, features_ref[...], 0, 0).astype(BF16).reshape(out_ref.shape)


def terms_kernel(kind, meta_ref, tiles_ref, cot_ref, token_ref, mine_ref, other_ref, acc_ref):
    del token_ref
    live, core = meta_ref[0], meta_ref[2]
    mine_ref[...] = jnp.zeros(mine_ref.shape, BF16)
    other_ref[...] = jnp.zeros(other_ref.shape, BF16)

    def each(k, act):
        block = meta_ref[SRC + k]
        pl.when((k < live) & (lax.div(block, 16) == kind))(lambda: act(lax.rem(block, 16)))

    for k in range(NT):
        @functools.partial(each, k)
        def _(block):
            acc_ref[block] = jnp.zeros(acc_ref.shape[1:], F32)
    for k in range(NT):
        @functools.partial(each, k)
        def _(block):
            acc_ref[block] += dot(tiles_ref[k], cot_ref[meta_ref[DST + k]], 0, 0)
    for k in range(NT):
        @functools.partial(each, k)
        def _(block):
            member, part = lax.div(block, 2), lax.rem(block, 2)
            y, same = lax.div(member, 2), lax.rem(member, 2) == core

            @pl.when(same)
            def _():
                mine_ref[y, part] = acc_ref[block].astype(BF16)

            @pl.when(jnp.logical_not(same))
            def _():
                other_ref[y, part] = acc_ref[block].astype(BF16)


def pair_kernel(meta_ref, mine_ref, came_ref, keep_ref, *out_refs):
    y = meta_ref[1]
    keep_ref[...] = mine_ref[y].astype(F32) + came_ref[y].astype(F32)
    for step, out_ref in enumerate(out_refs, 1):
        to = lax.rem(y + step, Y)
        out_ref[...] = (mine_ref[to].astype(F32) + came_ref[to].astype(F32)).astype(BF16)


def sum_kernel(keep_ref, came1_ref, came2_ref, came3_ref, token_ref, out_ref, out_token_ref):
    out_token_ref[...] = token_ref[...]
    terms = keep_ref[...]
    for came_ref in (came1_ref, came2_ref, came3_ref):
        terms += came_ref[...].astype(F32)
    out_ref[...] = terms.reshape(out_ref.shape)


def own_kernel(meta_ref, tiles_ref, cot_ref, source_ref, out_ref):
    live = meta_ref[0]
    out_ref[...] = jnp.zeros(out_ref.shape, F32)
    for k in range(NT):
        block = meta_ref[SRC + k]

        @pl.when((k < live) & (block < 16))
        def _():
            high, low = halves(dot(tiles_ref[k], cot_ref[meta_ref[DST + k]], 0, 0))
            source = source_ref[block]
            out_ref[...] += dot(source, high, 0, 0) + dot(source, low, 0, 0)


def side_kernel(keep_ref, came1_ref, came2_ref, came3_ref, far_ref, token_ref, high_ref, low_ref, out_ref):
    del token_ref
    terms = keep_ref[...]
    for came_ref in (came1_ref, came2_ref, came3_ref):
        terms += came_ref[...].astype(F32)
    bound = terms.reshape(2 * TILE, -1)
    rows, width = bound.shape
    column = lax.broadcasted_iota(jnp.int32, (rows, rows), 1)
    x, zl, zh, s = digits(rows, 0, (X, ZL, ZH, SLOTS))
    lines = rows // (X * ZL)
    order = permutation(((zh * X + x) * ZL + zl) * SLOTS + s == column)
    rows_out = dot(order, far_ref[...].reshape(rows, width)).astype(BF16)
    out_ref[:, :lines, :] = rows_out.reshape(X * ZL, lines, width)
    order = permutation(boundary_row(x, zh, zl, s) == column)
    high, low = halves(bound)
    high = dot(order, high).astype(BF16)
    high_ref[...] = high
    low_ref[...] = dot(order, low).astype(BF16)
    out_ref[:, lines:, :] = high.reshape(X * ZL, lines, width)


def mid_kernel(own_ref, high_ref, low_ref, side_ref, gw_ref, arrived_ref, token_ref):
    token_ref[...] = jnp.zeros(token_ref.shape, F32)
    rows, width = high_ref.shape
    arrived = side_ref[:, :rows // (X * ZL), :].reshape(rows, width)
    gw = own_ref[...] + dot(arrived, high_ref[...], 0, 0) + dot(arrived, low_ref[...], 0, 0)
    for c in range(CHUNKS):
        row, col = c // 2 * 8, c % 2 * 128
        gw_ref[c] = gw[row:row + 8, col:col + 128].astype(BF16)
    x, zl, zh, s = digits(rows, 1, (X, ZL, ZH, SLOTS))
    order = permutation(boundary_row(x, zh, zl, s) == lax.broadcasted_iota(jnp.int32, (rows, rows), 0))
    arrived_ref[...] = dot(order, arrived).astype(BF16)


def pack_kernel(side_ref, near_ref, out_ref):
    lines = out_ref.shape[1] // 2 - 4
    rows = ZH * lines
    zh, x, zl, s = digits(rows, 0, (ZH, X, ZL, SLOTS))
    order = permutation(((x * ZL + zl) * ZH + zh) * SLOTS + s == lax.broadcasted_iota(jnp.int32, (rows, rows), 1))
    side = dot(order, side_ref[:, rows // (X * ZL):, :].reshape(rows, -1)).astype(BF16)
    out_ref[:, :lines, :] = side[:, :128].reshape(ZH, lines, 128)
    out_ref[:, lines:2 * lines, :] = side[:, 128:].reshape(ZH, lines, 128)
    near = jnp.sum(near_ref[...].astype(F32), axis=0).astype(BF16)
    for z in range(ZH):
        out_ref[z, 2 * lines:, :] = near


def far_kernel(far_ref, token_ref, out_ref):
    del token_ref
    total = jnp.sum(far_ref[:, far_ref.shape[1] - 8:, :].astype(F32), axis=0)
    out_ref[...] = jnp.broadcast_to(total[None], out_ref.shape)


def back_kernel(rows_ref, count_ref, own_ref, far_ref, weight_ref, out_ref):
    rows = own_ref.shape[0]
    lines = far_ref.shape[1] // 2 - 4
    left = far_ref[:, :lines, :].reshape(ZH * lines, 128)
    right = far_ref[:, lines:2 * lines, :].reshape(ZH * lines, 128)
    total = own_ref[...] + dot(picks(rows, rows_ref, count_ref), jnp.concatenate([left, right], axis=1))
    high, low = halves(total)
    weight = weight_ref[...]
    out_ref[...] = dot(high, weight, 1, 1) + dot(low, weight, 1, 1)


def forward_kernel(meta_ref, tiles_ref, own_ref, bound_ref, weight_ref, out_ref, token_ref, acc_ref):
    live = meta_ref[0]
    token_ref[...] = jnp.zeros(token_ref.shape, F32)
    acc_ref[...] = jnp.zeros(acc_ref.shape, F32)
    for k in range(NT):
        block = meta_ref[SRC + k]

        @pl.when((k < live) & (block < 16))
        def _():
            acc_ref[meta_ref[DST + k]] += dot(tiles_ref[k], own_ref[block])

        @pl.when((k < live) & (block >= 16))
        def _():
            acc_ref[meta_ref[DST + k]] += dot(tiles_ref[k], bound_ref[block - 16])
    for t in range(2):
        out_ref[t] = dot(acc_ref[t].astype(BF16), weight_ref[...]).astype(BF16)


def per_device(
    features, tiles, tile_dst, tile_src, tile_count, send_rows, send_count, weight, cotangent
):
    rows, width = features.shape
    groups, slots = send_rows.shape[1:]
    lines = groups * slots // ZH
    shape = jax.ShapeDtypeStruct
    places = jnp.stack([lax.axis_index("y"), lax.axis_index("core")])
    meta = jnp.concatenate([tile_count, places, tile_src, tile_dst])
    send_rows = send_rows.transpose(0, 2, 1).reshape(slots, groups)

    cotangent = cotangent.reshape(2, TILE, width)
    blocked = (16, TILE, width)
    square = shape((rows, width), BF16)
    token = shape((8, 128), F32)

    all_own = lax.all_gather(features, DEV, axis=0, tiled=True).reshape(blocked)

    outgoing = call(pick_kernel, shape((ZH, lines, width), BF16), [VMEM] * 3, "pick", (), 60)(
        send_rows, send_count, features)
    landed = swap(outgoing, FAR)

    def exchange(kind, name, after):
        half = shape((Y, 2, TILE, width), BF16)
        part = shape((2, TILE, width), BF16)
        mine, other = call(
            functools.partial(terms_kernel, kind), (half, half), [SMEM, VMEM, VMEM, ANY], "terms_" + name,
            [pltpu.VMEM((16, TILE, width), F32)],
        )(meta, tiles, cotangent, after)
        came = shift(other, "core", 1, CORE)
        keep, *sent = call(
            pair_kernel, (shape(part.shape, F32), part, part, part), [SMEM] + [VMEM] * 2, "pair_" + name,
        )(meta, mine, came)
        return keep, [shift(block, "y", step, Y) for step, block in enumerate(sent, 1)]

    keep, sums = exchange(1, "bound", outgoing)
    gw_own = call(own_kernel, shape((width, width), F32), [SMEM] + [VMEM] * 3, "own")(meta, tiles, cotangent, all_own)
    high, low, side = call(
        side_kernel, (square, square, shape((X * ZL, 2 * rows // (X * ZL), width), BF16)), [VMEM] * 6, "side",
    )(keep, *sums, landed, all_own[0, :8, :128])
    side = swap(side, SIDE)
    gw, arrived, mid_token = call(
        mid_kernel, (shape((CHUNKS, 8, 128), BF16), square, token), [VMEM] * 4, "mid",
    )(gw_own, high, low, side)
    near = swap(gw, NEAR)
    packed = call(pack_kernel, shape((ZH, 2 * lines + 8, 128), BF16), [VMEM] * 2, "pack")(side, near)
    far = swap(packed, FAR)

    all_bound = lax.all_gather(arrived, DEV, axis=0, tiled=True).reshape(blocked)
    output, forward_token = call(
        forward_kernel, (shape((2, TILE, width), BF16), token), [SMEM] + [VMEM] * 4, "forward",
        [pltpu.VMEM((2, TILE, width), F32)],
    )(meta, tiles, all_own, all_bound, weight)
    keep, sums = exchange(0, "own", mid_token)
    own, last_token = call(sum_kernel, (shape((rows, width), F32), token), [VMEM] * 5, "sum")(
        keep, *sums, forward_token)

    spread = call(far_kernel, shape((CHUNKS, 8, 128), F32), [VMEM] * 2, "far")(far, last_token)
    grad_weight = swap(spread, NEAR).reshape(width // 8, 2, 8, 128).transpose(0, 2, 1, 3).reshape(width, width)
    grad_features = call(back_kernel, shape((rows, width), F32), [VMEM] * 5, "back")(
        send_rows, send_count, own, far, weight)
    return output.reshape(rows, width), grad_features, grad_weight


def solution(mesh):
    fine = Mesh(mesh.devices.reshape(SIZES), AXES)
    split = [P(AXES)] * 7
    return jax.shard_map(
        per_device,
        mesh=fine,
        in_specs=(*split, P(), P(AXES)),
        out_specs=(P(AXES), P(AXES), P()),
        check_vma=False,
    )
```

```python
import functools

import jax
import jax.numpy as jnp
from jax import lax
from jax.experimental import pallas as pl
from jax.experimental.pallas import tpu as pltpu
from jax.sharding import Mesh, PartitionSpec as P

AXES = ("x", "zh", "zl", "y", "core")
SIZES = (4, 16, 2, 4, 2)
SLOTS = 2
X, ZH, ZL, Y, CORE = SIZES
DEV = ("y", "core")
SIDE = ("x", "zl")
NEAR = ("x", "zl", "y", "core")
FAR = "zh"
TILE = 128
NT = 8
CHUNKS = 64
SRC = 3
DST = SRC + NT

F32 = jnp.float32
BF16 = jnp.bfloat16
SMEM = pl.BlockSpec(memory_space=pltpu.SMEM)
ANY = pl.BlockSpec(memory_space=pl.ANY)
VMEM = pl.BlockSpec(memory_space=pltpu.VMEM)


def swap(x, axes):
    return lax.all_to_all(x, axes, split_axis=0, concat_axis=0, tiled=True)


def shift(x, axis, step, size):
    return lax.ppermute(x, axis, [(i, (i + step) % size) for i in range(size)])


def dot(a, b, da=1, db=0):
    return lax.dot_general(a, b, (((da,), (db,)), ((), ())), preferred_element_type=F32)


def halves(x):
    high = x.astype(BF16)
    return high, (x - high.astype(F32)).astype(BF16)


def call(kernel, out_shape, in_specs, name, scratch=(), mebibytes=24):
    out_specs = (VMEM,) * len(out_shape) if isinstance(out_shape, tuple) else VMEM
    return pl.pallas_call(
        kernel, out_shape=out_shape, in_specs=in_specs, out_specs=out_specs,
        scratch_shapes=scratch, name=name,
        compiler_params=pltpu.CompilerParams(vmem_limit_bytes=mebibytes * 1024 * 1024),
    )


def digits(count, dim, sizes):
    left = lax.broadcasted_iota(jnp.int32, (count, 1) if dim == 0 else (1, count), dim)
    found = []
    for size in reversed(sizes):
        found.append(left & (size - 1))
        left = left >> (size.bit_length() - 1)
    return found[::-1]


def boundary_row(x, zh, zl, s):
    return ((x * ZH + zh) * ZL + zl) * SLOTS + s


def permutation(match):
    return match.astype(F32).astype(BF16)


def picks(rows, rows_ref, count_ref):
    groups = count_ref.shape[1]
    places = lax.broadcasted_iota(jnp.int32, (rows, groups), 0)
    found = []
    for slot in range(SLOTS):
        live = count_ref[...] > slot
        wanted = jnp.where(live, rows_ref[slot:slot + 1, :], -1)
        found.append(permutation(places == wanted))
    count = groups * SLOTS
    zh, x, zl, s = digits(count, 1, (ZH, X, ZL, SLOTS))
    order = permutation(s * groups + (x * ZH + zh) * ZL + zl == lax.broadcasted_iota(jnp.int32, (count, count), 0))
    return dot(jnp.concatenate(found, axis=1), order).astype(BF16)


def pick_kernel(rows_ref, count_ref, features_ref, out_ref):
    wanted = picks(features_ref.shape[0], rows_ref, count_ref)
    out_ref[...] = dot(wanted, features_ref[...], 0, 0).astype(BF16).reshape(out_ref.shape)


def terms_kernel(kind, meta_ref, tiles_ref, cot_ref, token_ref, mine_ref, other_ref, acc_ref):
    del token_ref
    live, core = meta_ref[0], meta_ref[2]
    mine_ref[...] = jnp.zeros(mine_ref.shape, BF16)
    other_ref[...] = jnp.zeros(other_ref.shape, BF16)

    def each(k, act):
        block = meta_ref[SRC + k]
        pl.when((k < live) & (lax.div(block, 16) == kind))(lambda: act(lax.rem(block, 16)))

    for k in range(NT):
        @functools.partial(each, k)
        def _(block):
            acc_ref[block] = jnp.zeros(acc_ref.shape[1:], F32)
    for k in range(NT):
        @functools.partial(each, k)
        def _(block):
            acc_ref[block] += dot(tiles_ref[k], cot_ref[meta_ref[DST + k]], 0, 0)
    for k in range(NT):
        @functools.partial(each, k)
        def _(block):
            member, part = lax.div(block, 2), lax.rem(block, 2)
            y, same = lax.div(member, 2), lax.rem(member, 2) == core

            @pl.when(same)
            def _():
                mine_ref[y, part] = acc_ref[block].astype(BF16)

            @pl.when(jnp.logical_not(same))
            def _():
                other_ref[y, part] = acc_ref[block].astype(BF16)


def pair_kernel(meta_ref, mine_ref, came_ref, keep_ref, *out_refs):
    y = meta_ref[1]
    keep_ref[...] = mine_ref[y].astype(F32) + came_ref[y].astype(F32)
    for step, out_ref in enumerate(out_refs, 1):
        to = lax.rem(y + step, Y)
        out_ref[...] = (mine_ref[to].astype(F32) + came_ref[to].astype(F32)).astype(BF16)


def sum_kernel(keep_ref, came1_ref, came2_ref, came3_ref, token_ref, out_ref, out_token_ref):
    out_token_ref[...] = token_ref[...]
    terms = keep_ref[...]
    for came_ref in (came1_ref, came2_ref, came3_ref):
        terms += came_ref[...].astype(F32)
    out_ref[...] = terms.reshape(out_ref.shape)


def own_kernel(meta_ref, tiles_ref, cot_ref, source_ref, out_ref):
    live = meta_ref[0]
    out_ref[...] = jnp.zeros(out_ref.shape, F32)
    for k in range(NT):
        block = meta_ref[SRC + k]

        @pl.when((k < live) & (block < 16))
        def _():
            high, low = halves(dot(tiles_ref[k], cot_ref[meta_ref[DST + k]], 0, 0))
            source = source_ref[block]
            out_ref[...] += dot(source, high, 0, 0) + dot(source, low, 0, 0)


def side_kernel(keep_ref, came1_ref, came2_ref, came3_ref, far_ref, token_ref, high_ref, low_ref, out_ref):
    del token_ref
    terms = keep_ref[...]
    for came_ref in (came1_ref, came2_ref, came3_ref):
        terms += came_ref[...].astype(F32)
    bound = terms.reshape(2 * TILE, -1)
    rows, width = bound.shape
    column = lax.broadcasted_iota(jnp.int32, (rows, rows), 1)
    x, zl, zh, s = digits(rows, 0, (X, ZL, ZH, SLOTS))
    lines = rows // (X * ZL)
    order = permutation(((zh * X + x) * ZL + zl) * SLOTS + s == column)
    rows_out = dot(order, far_ref[...].reshape(rows, width)).astype(BF16)
    out_ref[:, :lines, :] = rows_out.reshape(X * ZL, lines, width)
    order = permutation(boundary_row(x, zh, zl, s) == column)
    high, low = halves(bound)
    high = dot(order, high).astype(BF16)
    high_ref[...] = high
    low_ref[...] = dot(order, low).astype(BF16)
    out_ref[:, lines:, :] = high.reshape(X * ZL, lines, width)


def mid_kernel(own_ref, high_ref, low_ref, side_ref, gw_ref, arrived_ref, token_ref):
    token_ref[...] = jnp.zeros(token_ref.shape, F32)
    rows, width = high_ref.shape
    arrived = side_ref[:, :rows // (X * ZL), :].reshape(rows, width)
    gw = own_ref[...] + dot(arrived, high_ref[...], 0, 0) + dot(arrived, low_ref[...], 0, 0)
    for c in range(CHUNKS):
        row, col = c // 2 * 8, c % 2 * 128
        gw_ref[c] = gw[row:row + 8, col:col + 128].astype(BF16)
    x, zl, zh, s = digits(rows, 1, (X, ZL, ZH, SLOTS))
    order = permutation(boundary_row(x, zh, zl, s) == lax.broadcasted_iota(jnp.int32, (rows, rows), 0))
    arrived_ref[...] = dot(order, arrived).astype(BF16)


def pack_kernel(side_ref, near_ref, out_ref):
    lines = out_ref.shape[1] // 2 - 4
    rows = ZH * lines
    zh, x, zl, s = digits(rows, 0, (ZH, X, ZL, SLOTS))
    order = permutation(((x * ZL + zl) * ZH + zh) * SLOTS + s == lax.broadcasted_iota(jnp.int32, (rows, rows), 1))
    side = dot(order, side_ref[:, rows // (X * ZL):, :].reshape(rows, -1)).astype(BF16)
    out_ref[:, :lines, :] = side[:, :128].reshape(ZH, lines, 128)
    out_ref[:, lines:2 * lines, :] = side[:, 128:].reshape(ZH, lines, 128)
    near = jnp.sum(near_ref[...].astype(F32), axis=0).astype(BF16)
    for z in range(ZH):
        out_ref[z, 2 * lines:, :] = near


def far_kernel(far_ref, token_ref, out_ref):
    del token_ref
    total = jnp.sum(far_ref[:, far_ref.shape[1] - 8:, :].astype(F32), axis=0)
    out_ref[...] = jnp.broadcast_to(total[None], out_ref.shape)


def back_kernel(rows_ref, count_ref, own_ref, far_ref, weight_ref, out_ref):
    rows = own_ref.shape[0]
    lines = far_ref.shape[1] // 2 - 4
    left = far_ref[:, :lines, :].reshape(ZH * lines, 128)
    right = far_ref[:, lines:2 * lines, :].reshape(ZH * lines, 128)
    total = own_ref[...] + dot(picks(rows, rows_ref, count_ref), jnp.concatenate([left, right], axis=1))
    high, low = halves(total)
    weight = weight_ref[...]
    out_ref[...] = dot(high, weight, 1, 1) + dot(low, weight, 1, 1)


def forward_kernel(meta_ref, tiles_ref, own_ref, bound_ref, weight_ref, out_ref, token_ref, acc_ref):
    live = meta_ref[0]
    token_ref[...] = jnp.zeros(token_ref.shape, F32)
    acc_ref[...] = jnp.zeros(acc_ref.shape, F32)
    for k in range(NT):
        block = meta_ref[SRC + k]

        @pl.when((k < live) & (block < 16))
        def _():
            acc_ref[meta_ref[DST + k]] += dot(tiles_ref[k], own_ref[block])

        @pl.when((k < live) & (block >= 16))
        def _():
            acc_ref[meta_ref[DST + k]] += dot(tiles_ref[k], bound_ref[block - 16])
    for t in range(2):
        out_ref[t] = dot(acc_ref[t].astype(BF16), weight_ref[...]).astype(BF16)


def per_device(
    features, tiles, tile_dst, tile_src, tile_count, send_rows, send_count, weight, cotangent
):
    rows, width = features.shape
    groups, slots = send_rows.shape[1:]
    lines = groups * slots // ZH
    shape = jax.ShapeDtypeStruct
    places = jnp.stack([lax.axis_index("y"), lax.axis_index("core")])
    meta = jnp.concatenate([tile_count, places, tile_src, tile_dst])
    send_rows = send_rows.transpose(0, 2, 1).reshape(slots, groups)

    cotangent = cotangent.reshape(2, TILE, width)
    blocked = (16, TILE, width)
    square = shape((rows, width), BF16)
    token = shape((8, 128), F32)

    all_own = lax.all_gather(features, DEV, axis=0, tiled=True).reshape(blocked)

    outgoing = call(pick_kernel, shape((ZH, lines, width), BF16), [VMEM] * 3, "pick", (), 60)(
        send_rows, send_count, features)
    landed = swap(outgoing, FAR)

    def exchange(kind, name, after):
        half = shape((Y, 2, TILE, width), BF16)
        part = shape((2, TILE, width), BF16)
        mine, other = call(
            functools.partial(terms_kernel, kind), (half, half), [SMEM, VMEM, VMEM, ANY], "terms_" + name,
            [pltpu.VMEM((16, TILE, width), F32)],
        )(meta, tiles, cotangent, after)
        came = shift(other, "core", 1, CORE)
        keep, *sent = call(
            pair_kernel, (shape(part.shape, F32), part, part, part), [SMEM] + [VMEM] * 2, "pair_" + name,
        )(meta, mine, came)
        return keep, [shift(block, "y", step, Y) for step, block in enumerate(sent, 1)]

    keep, sums = exchange(1, "bound", outgoing)
    gw_own = call(own_kernel, shape((width, width), F32), [SMEM] + [VMEM] * 3, "own")(meta, tiles, cotangent, all_own)
    high, low, side = call(
        side_kernel, (square, square, shape((X * ZL, 2 * rows // (X * ZL), width), BF16)), [VMEM] * 6, "side",
    )(keep, *sums, landed, all_own[0, :8, :128])
    side = swap(side, SIDE)
    gw, arrived, mid_token = call(
        mid_kernel, (shape((CHUNKS, 8, 128), BF16), square, token), [VMEM] * 4, "mid",
    )(gw_own, high, low, side)
    near = swap(gw, NEAR)
    packed = call(pack_kernel, shape((ZH, 2 * lines + 8, 128), BF16), [VMEM] * 2, "pack")(side, near)
    far = swap(packed, FAR)

    all_bound = lax.all_gather(arrived, DEV, axis=0, tiled=True).reshape(blocked)
    output, forward_token = call(
        forward_kernel, (shape((2, TILE, width), BF16), token), [SMEM] + [VMEM] * 4, "forward",
        [pltpu.VMEM((2, TILE, width), F32)],
    )(meta, tiles, all_own, all_bound, weight)
    keep, sums = exchange(0, "own", mid_token)
    own, last_token = call(sum_kernel, (shape((rows, width), F32), token), [VMEM] * 5, "sum")(
        keep, *sums, forward_token)

    spread = call(far_kernel, shape((CHUNKS, 8, 128), F32), [VMEM] * 2, "far")(far, last_token)
    grad_weight = swap(spread, NEAR).reshape(width // 8, 2, 8, 128).transpose(0, 2, 1, 3).reshape(width, width)
    grad_features = call(back_kernel, shape((rows, width), F32), [VMEM] * 5, "back")(
        send_rows, send_count, own, far, weight)
    return output.reshape(rows, width), grad_features, grad_weight


def solution(mesh):
    fine = Mesh(mesh.devices.reshape(SIZES), AXES)
    split = [P(AXES)] * 7
    return jax.shard_map(
        per_device,
        mesh=fine,
        in_specs=(*split, P(), P(AXES)),
        out_specs=(P(AXES), P(AXES), P()),
        check_vma=False,
    )
```
